128 devices in a mesh: dp: 8 (over x, core), tensor: 16 (over z, y).
Axes of the slice: x: 4, y: 4, z: 4, core: 2. Of those that a mesh axis runs over, the one named last changes fastest.
Arguments:
- gate_grad: float32 [8, 256, 28672], P('dp', 'tensor'), may hold values from -6 to 6
- up_grad: float32 [8, 256, 28672], P('dp', 'tensor'), may hold values from -6 to 6
- down_grad: float32 [8, 256, 8192], P('dp', 'tensor'), may hold values from -6 to 6
- gate_error: bfloat16 [8, 256, 28672], P('dp', 'tensor'), may hold values from -4 to 4
- up_error: bfloat16 [8, 256, 28672], P('dp', 'tensor'), may hold values from -4 to 4
- down_error: bfloat16 [8, 256, 8192], P('dp', 'tensor'), may hold values from -4 to 4
- gate_right: float32 [4, 28672], replicated, may hold values from -0.03125 to 0.03125
- up_right: float32 [4, 28672], replicated, may hold values from -0.03125 to 0.03125
- down_right: float32 [4, 8192], replicated, may hold values from -0.0625 to 0.0625
Outputs:
- gate_left: float32 [4, 256], P(None, 'tensor')
- up_left: float32 [4, 256], P(None, 'tensor')
- down_left: float32 [4, 256], P(None, 'tensor')
- gate_right_next: float32 [4, 28672], replicated
- up_right_next: float32 [4, 28672], replicated
- down_right_next: float32 [4, 8192], replicated
- gate_error_next: bfloat16 [8, 256, 28672], P('dp', 'tensor')
- up_error_next: bfloat16 [8, 256, 28672], P('dp', 'tensor')
- down_error_next: bfloat16 [8, 256, 8192], P('dp', 'tensor')
The draws below stay inside these ranges and needn't reach their ends.
All inputs are finite; a program needn't handle non-finite values.
Results may differ from the reference program's by a relative error of at most 0.001.
Values sent between devices are 32-bit elements; how exact they have to be, the bound alone decides.
No kernel may reach another device: no remote copies, remote signals or barrier semaphores. Data moves between devices by JAX's collectives and lax.ppermute only.
A program may use at most 128 MiB of HBM per device.

```python
import jax
import jax.numpy as jnp
from jax import lax

D = 8192
FF = 28672
RANK = 4
ROWS = 256
N_DP = 8


def block_levels(stream_key, dims, shards, least, top_value):
    def one(position, parts):
        draws = jax.random.uniform(jax.random.fold_in(jax.random.fold_in(stream_key, 6), position), (parts,), jnp.float32, least / len(shards), top_value / len(shards))
        return jnp.repeat(jnp.exp(draws), dims[position] // parts).reshape((-1,) + (1,) * (len(dims) - position - 1))

    factor_of = one(*shards[0])
    for cut in shards[1:]:
        factor_of = factor_of * one(*cut)
    return factor_of


def bell_draw(stream_key, shape, scale, limit, shards=(), dtype=jnp.bfloat16):
    values = jax.random.normal(stream_key, shape, jnp.float32) * scale
    if len(shards) > 0:
        values = block_levels(stream_key, shape, shards, -0.22, 0.18) * values
    return jnp.clip(values, min=-limit, max=limit).astype(dtype)


def setup_inputs(seed: int = 0) -> dict:
    key_list = jax.random.split(jax.random.key(seed), 10)
    return {
        "gate_grad": bell_draw(key_list[0], (N_DP, ROWS, FF), 1.0, 6.0, ((0, 8), (1, 16)), jnp.float32),
        "up_grad": bell_draw(key_list[1], (N_DP, ROWS, FF), 1.0, 6.0, ((0, 8), (1, 16)), jnp.float32),
        "down_grad": bell_draw(key_list[2], (N_DP, ROWS, D), 1.0, 6.0, ((0, 8), (1, 16)), jnp.float32),
        "gate_error": bell_draw(key_list[3], (N_DP, ROWS, FF), 0.5, 4.0, ((0, 8), (1, 16))),
        "up_error": bell_draw(key_list[4], (N_DP, ROWS, FF), 0.5, 4.0, ((0, 8), (1, 16))),
        "down_error": bell_draw(key_list[5], (N_DP, ROWS, D), 0.5, 4.0, ((0, 8), (1, 16))),
        "gate_right": bell_draw(key_list[6], (RANK, FF), FF ** -0.5, 0.03125, (), jnp.float32),
        "up_right": bell_draw(key_list[7], (RANK, FF), FF ** -0.5, 0.03125, (), jnp.float32),
        "down_right": bell_draw(key_list[8], (RANK, D), D ** -0.5, 0.0625, (), jnp.float32),
    }


def forward_solve(factor, left_sum):
    rows_out = []
    for row_index in range(left_sum.shape[0]):
        current = left_sum[row_index]
        for earlier_index in range(row_index):
            current = current - factor[row_index, earlier_index] * rows_out[earlier_index]
        rows_out.append(current / factor[row_index, row_index])
    return jnp.stack(rows_out)

def compress(grad, error, right):
    highest = lax.Precision.HIGHEST
    merged = grad + error.astype(jnp.float32)
    replicas = grad.shape[0]
    left_sum = jnp.einsum('rnc,kc->kn', merged, right, precision=highest) / replicas
    gram = jnp.dot(left_sum, left_sum.T, precision=highest)
    factor = jnp.linalg.cholesky(gram)
    left = forward_solve(factor, left_sum)
    right_next = jnp.einsum('rnc,kn->kc', merged, left, precision=highest) / replicas
    approx = jnp.dot(left.T, right_next, precision=highest)
    error_next = (merged - approx[None]).astype(jnp.bfloat16)
    return (left, right_next, error_next)

def reference(gate_grad, up_grad, down_grad, gate_error, up_error, down_error, gate_right, up_right, down_right):
    gate_left, gate_next, gate_err = compress(gate_grad, gate_error, gate_right)
    up_left, up_next, up_err = compress(up_grad, up_error, up_right)
    down_left, down_next, down_err = compress(down_grad, down_error, down_right)
    return (gate_left, up_left, down_left, gate_next, up_next, down_next, gate_err, up_err, down_err)
```

```python
import functools

import jax
import jax.numpy as jnp
from jax import lax
from jax.experimental import pallas as pl
from jax.experimental.pallas import tpu as pltpu
from jax.sharding import PartitionSpec as P

F32 = jnp.float32
BF16 = jnp.bfloat16
RANK = 4
ROWS = 16
LANES = 128
COLS = (28672, 28672, 8192)
BLOCK = 4 * LANES
PIECE = 4096
CHIPS = 64
BLOCK_ROWS = 17
HALF_BLOCKS = tuple(c // 2 // BLOCK for c in COLS)
FIRST_BLOCK = (0, HALF_BLOCKS[0], HALF_BLOCKS[0] + HALF_BLOCKS[1])


def lane_iota(rows):
    return lax.broadcasted_iota(jnp.int32, (rows, LANES), 1)


def merge_kernel(*refs):
    grads, errors, rights = refs[0:3], refs[3:6], refs[6:9]
    merged, partial = refs[9:12], refs[12]
    gbuf, ebuf, rbuf, sems = refs[13:16], refs[16:19], refs[19:22], refs[22]
    copies = []
    index = 0
    for m in range(3):
        for piece in range(COLS[m] // PIECE):
            cols = pl.ds(piece * PIECE, PIECE)
            group = [
                pltpu.make_async_copy(grads[m].at[0, :, cols], gbuf[m].at[:, cols], sems.at[index, 0]),
                pltpu.make_async_copy(errors[m].at[0, :, cols], ebuf[m].at[:, cols], sems.at[index, 1]),
                pltpu.make_async_copy(rights[m].at[:, cols], rbuf[m].at[:, cols], sems.at[index, 2]),
            ]
            for copy in group:
                copy.start()
            copies.append((m, piece, group))
            index += 1
    lanes = lane_iota(ROWS)
    result = jnp.zeros((ROWS, LANES), F32)
    totals = None
    for m, piece, group in copies:
        if piece == 0:
            totals = tuple(jnp.zeros((ROWS, LANES), F32) for _ in range(RANK))
        for copy in group:
            copy.wait()

        def step(j, acc, m=m, piece=piece):
            cols = pl.ds(pl.multiple_of(piece * PIECE + j * LANES, LANES), LANES)
            value = gbuf[m][:, cols] + ebuf[m][:, cols].astype(F32)
            merged[m][:, cols] = value
            return tuple(acc[i] + value * rbuf[m][i : i + 1, cols] for i in range(RANK))

        totals = lax.fori_loop(0, PIECE // LANES, step, totals, unroll=4)
        if piece == COLS[m] // PIECE - 1:
            for i in range(RANK):
                column = jnp.sum(totals[i], axis=1, keepdims=True)
                result = jnp.where(lanes == m * RANK + i, column, result)
    for k in range(8):
        partial[k] = result


def sum_replicas(gathered):
    return (
        ((gathered[0] + gathered[1]) + (gathered[2] + gathered[3]))
        + ((gathered[4] + gathered[5]) + (gathered[6] + gathered[7]))
    ) * 0.125


def fold(a, b, distance):
    mask = (lax.broadcasted_iota(jnp.int32, (8, LANES), 0) & distance) == 0
    return jnp.where(mask, a, b) + pltpu.roll(jnp.where(mask, b, a), 8 - distance, 0)


def product_kernel(own, gathered, *refs):
    merged, out = refs[0:3], refs[3]
    core = lax.rem(lax.axis_index("dp"), 2)
    half = core if own else 1 - core
    left = sum_replicas(gathered)
    lanes = lane_iota(1)
    gram = jnp.zeros((1, LANES), F32)
    for shift in range(RANK):
        other = left if shift == 0 else pltpu.roll(left, LANES - shift, 1)
        row = jnp.where(lanes < 3 * RANK, jnp.sum(left * other, axis=0, keepdims=True), 0.0)
        gram = gram + (row if shift == 0 else pltpu.roll(row, 16 * shift, 1))
    for m in range(3):
        columns = [
            jnp.broadcast_to(left[:, m * RANK + i : m * RANK + i + 1], (ROWS, LANES)) for i in range(RANK)
        ]

        def step(block, carry, m=m, columns=columns):
            first = half * (COLS[m] // 2) + block * BLOCK
            row = (FIRST_BLOCK[m] + block) * BLOCK_ROWS
            for pair in range(2):
                terms = []
                for b in range(2):
                    cols = pl.ds(pl.multiple_of(first + (2 * pair + b) * LANES, LANES), LANES)
                    value = merged[m][:, cols]
                    for i in range(RANK):
                        product = columns[i] * value
                        terms.append(product[:8] + product[8:])
                ones = [fold(terms[2 * k], terms[2 * k + 1], 1) for k in range(4)]
                twos = [fold(ones[2 * k], ones[2 * k + 1], 2) for k in range(2)]
                out[pl.ds(row + 8 * pair, 8), :] = fold(twos[0], twos[1], 4)
            out[pl.ds(row + 16, 1), :] = gram
            return carry

        lax.fori_loop(0, HALF_BLOCKS[m], step, 0, unroll=2)


def solve_kernel(blocks, gathered, copies, left_out, scratch):
    total = [jnp.zeros((16, LANES), F32) for _ in range(4)]
    grams = [jnp.zeros((1, LANES), F32) for _ in range(4)]
    for k in range(CHIPS):
        total[k % 4] = total[k % 4] + blocks[k * BLOCK_ROWS : k * BLOCK_ROWS + 16, :]
        grams[k % 4] = grams[k % 4] + blocks[k * BLOCK_ROWS + 16 : k * BLOCK_ROWS + 17, :]
    scratch[...] = (total[0] + total[1]) + (total[2] + total[3])
    gram = ((grams[0] + grams[1]) + (grams[2] + grams[3])) * 0.125

    def entry(i, j):
        shift = 16 * (i - j) + j
        return gram if shift == 0 else pltpu.roll(gram, LANES - shift, 1)

    factor = {}
    for j in range(RANK):
        for i in range(j, RANK):
            value = entry(i, j)
            for k in range(j):
                value = value - factor[i, k] * factor[j, k]
            factor[i, j] = jnp.sqrt(value) if i == j else value / factor[j, j]

    left_sum = sum_replicas(gathered)
    lanes = lane_iota(ROWS)
    valid = (lanes < 3 * RANK) & ((lanes & 3) == 0)
    rows, left = [], jnp.zeros((ROWS, LANES), F32)
    for i in range(RANK):
        current = left_sum if i == 0 else pltpu.roll(left_sum, LANES - i, 1)
        for j in range(i):
            current = current - factor[i, j] * rows[j]
        rows.append(current / factor[i, i])
        kept = jnp.where(valid, rows[i], 0.0)
        left = left + (kept if i == 0 else pltpu.roll(kept, i, 1))
    left_out[...] = left

    mine = (lax.axis_index("dp") // 2) * 16 + lax.axis_index("tensor")
    matrix = jnp.where(mine < FIRST_BLOCK[1], 0, jnp.where(mine < FIRST_BLOCK[2], 1, 2))
    one_lane = lane_iota(1) == matrix * RANK
    nexts = []
    for i in range(RANK):
        current = scratch[pl.ds(i, 4, stride=4), :] * 0.125
        for j in range(i):
            value = jnp.sum(jnp.where(one_lane, factor[i, j], 0.0), axis=1, keepdims=True)
            current = current - value * nexts[j]
        value = jnp.sum(jnp.where(one_lane, factor[i, i], 0.0), axis=1, keepdims=True)
        nexts.append(current / value)
    for i in range(RANK):
        scratch[pl.ds(i, 4, stride=4), :] = nexts[i]
    block = scratch[...]
    for k in range(CHIPS):
        copies[k] = block


OUT_PIECES = (4, 4, 1)


def finish_kernel(own, *refs):
    if own:
        rows, left_ref = refs[0:2]
        merged = refs[2:5]
        nexts, errors, lefts = refs[5:8], refs[8:11], refs[11:14]
        nbuf, ebuf, square, sems = refs[14:17], refs[17:20], refs[20], refs[21]
    else:
        rows, left_ref = refs[0:2]
        merged = refs[2:5]
        nexts, errors = refs[11:14], refs[14:17]
        nbuf, ebuf, sems = refs[17:20], refs[20:23], refs[23]
    core = lax.rem(lax.axis_index("dp"), 2)
    half = core if own else 1 - core
    left = left_ref[...]
    copies = []
    index = 0
    for m in range(3):
        size = COLS[m] // 2 // OUT_PIECES[m]
        columns = [
            jnp.broadcast_to(left[:, m * RANK + i : m * RANK + i + 1], (ROWS, LANES)) for i in range(RANK)
        ]
        for piece in range(OUT_PIECES[m]):

            def step(j, carry, m=m, piece=piece, columns=columns, size=size):
                local = pl.multiple_of(piece * size + j * LANES, LANES)
                value = merged[m][:, pl.ds(pl.multiple_of(half * (COLS[m] // 2) + local, LANES), LANES)]
                row = FIRST_BLOCK[m] * 16 + piece * (size // LANES) * RANK + j * RANK
                nbuf[m][:, pl.ds(local, LANES)] = rows[pl.ds(row, RANK), :]
                approx = columns[0] * rows[pl.ds(row, 1), :]
                for i in range(1, RANK):
                    approx = approx + columns[i] * rows[pl.ds(row + i, 1), :]
                ebuf[m][:, pl.ds(local, LANES)] = (value - approx).astype(BF16)
                return carry

            lax.fori_loop(0, size // LANES, step, 0, unroll=4)
            here = pl.ds(piece * size, size)
            there = pl.ds(pl.multiple_of(half * (COLS[m] // 2) + piece * size, LANES), size)
            for copy in (
                pltpu.make_async_copy(ebuf[m].at[:, here], errors[m].at[0, :, there], sems.at[index, 0]),
                pltpu.make_async_copy(nbuf[m].at[:, here], nexts[m].at[:, there], sems.at[index, 1]),
            ):
                copy.start()
                copies.append(copy)
            index += 1
    if own:
        square[...] = jnp.zeros((LANES, LANES), F32)
        square[0:ROWS, :] = left
        turned = square[...].T
        for m in range(3):
            lefts[m][...] = turned[m * RANK : (m + 1) * RANK, 0:ROWS]
    for copy in copies:
        copy.wait()


ANY = pl.BlockSpec(memory_space=pl.ANY)
VMEM = pl.BlockSpec(memory_space=pltpu.VMEM)
PARAMS = pltpu.CompilerParams(vmem_limit_bytes=24 * 2**20)


def cost(flops, size):
    return pl.CostEstimate(flops=flops, bytes_accessed=size, transcendentals=0)


def per_device(*args):
    grads, errors, rights = args[0:3], args[3:6], args[6:9]
    pieces = sum(COLS) // PIECE
    *merged, partial = pl.pallas_call(
        merge_kernel,
        out_shape=[pltpu.VMEM((ROWS, c), F32) for c in COLS] + [jax.ShapeDtypeStruct((8, ROWS, LANES), F32)],
        in_specs=[ANY] * 9,
        out_specs=[VMEM] * 4,
        scratch_shapes=[pltpu.VMEM((ROWS, c), F32) for c in COLS]
        + [pltpu.VMEM((ROWS, c), BF16) for c in COLS]
        + [pltpu.VMEM((RANK, c), F32) for c in COLS]
        + [pltpu.SemaphoreType.DMA((pieces, 3))],
        compiler_params=PARAMS,
        cost_estimate=cost(10**7, 7 * 2**20),
    )(*grads, *errors, *rights)
    gathered = lax.all_to_all(partial, "dp", 0, 0, tiled=True)

    rows = CHIPS * BLOCK_ROWS

    def product(own):
        return pl.pallas_call(
            functools.partial(product_kernel, own),
            out_shape=jax.ShapeDtypeStruct((rows, LANES), F32),
            in_specs=[VMEM] * 4,
            out_specs=VMEM,
            compiler_params=PARAMS,
            cost_estimate=cost(10**7, 5 * 2**20),
        )(gathered, *merged)

    swap = [(i, i ^ 1) for i in range(8)]
    sent = product(False)
    received = lax.ppermute(sent, "dp", swap)
    chip_sum = product(True) + received
    both = ("dp", "tensor")
    chips = [[(2 * x + core) * 16 + t for x in range(4) for t in range(16)] for core in range(2)]
    blocks = lax.all_to_all(
        chip_sum.reshape(CHIPS, 1, BLOCK_ROWS * LANES), both, 0, 0, tiled=True, axis_index_groups=chips
    ).reshape(rows, LANES)

    copies, left = pl.pallas_call(
        solve_kernel,
        out_shape=[
            jax.ShapeDtypeStruct((CHIPS, 16, LANES), F32),
            jax.ShapeDtypeStruct((ROWS, LANES), F32),
        ],
        in_specs=[VMEM] * 2,
        out_specs=[VMEM] * 2,
        scratch_shapes=[pltpu.VMEM((16, LANES), F32)],
        compiler_params=PARAMS,
        cost_estimate=cost(10**6, 2**20),
    )(blocks, gathered)
    mine = lax.all_to_all(copies, both, 0, 0, tiled=True, axis_index_groups=chips).reshape(CHIPS * 16, LANES)
    theirs = lax.ppermute(mine, "dp", swap)

    next_shapes = [jax.ShapeDtypeStruct((RANK, c), F32) for c in COLS]
    error_shapes = [jax.ShapeDtypeStruct((1, ROWS, c), BF16) for c in COLS]
    left_shapes = [jax.ShapeDtypeStruct((RANK, ROWS), F32)] * 3
    scratch = [pltpu.VMEM((RANK, c // 2), F32) for c in COLS] + [pltpu.VMEM((ROWS, c // 2), BF16) for c in COLS]
    sems = pltpu.SemaphoreType.DMA((sum(OUT_PIECES), 2))
    first = pl.pallas_call(
        functools.partial(finish_kernel, True),
        out_shape=next_shapes + error_shapes + left_shapes,
        in_specs=[VMEM] * 5,
        out_specs=[ANY] * 6 + [VMEM] * 3,
        scratch_shapes=scratch + [pltpu.VMEM((LANES, LANES), F32), sems],
        compiler_params=PARAMS,
        cost_estimate=cost(10**7, 4 * 2**20),
    )(mine, left, *merged)
    lefts = first[6:9]
    second = pl.pallas_call(
        functools.partial(finish_kernel, False),
        out_shape=next_shapes + error_shapes,
        in_specs=[VMEM] * 5 + [ANY] * 6,
        out_specs=[ANY] * 6,
        scratch_shapes=scratch + [sems],
        input_output_aliases={5 + k: k for k in range(6)},
        compiler_params=PARAMS,
        cost_estimate=cost(10**7, 4 * 2**20),
    )(theirs, left, *merged, *first[0:6])
    return (*lefts, *second)


def solution(mesh):
    cut = P("dp", "tensor", None)
    return jax.shard_map(
        per_device,
        mesh=mesh,
        in_specs=(cut,) * 6 + (P(),) * 3,
        out_specs=(P(None, "tensor"),) * 3 + (P(),) * 3 + (cut,) * 3,
        check_vma=False,
    )
```

```python
import functools

import jax
import jax.numpy as jnp
from jax import lax
from jax.experimental import pallas as pl
from jax.experimental.pallas import tpu as pltpu
from jax.sharding import PartitionSpec as P

F32 = jnp.float32
BF16 = jnp.bfloat16
RANK = 4
ROWS = 16
LANES = 128
COLS = (28672, 28672, 8192)
BLOCK = 4 * LANES
PIECE = 4096
CHIPS = 64
BLOCK_ROWS = 17
HALF_BLOCKS = tuple(c // 2 // BLOCK for c in COLS)
FIRST_BLOCK = (0, HALF_BLOCKS[0], HALF_BLOCKS[0] + HALF_BLOCKS[1])


def lane_iota(rows):
    return lax.broadcasted_iota(jnp.int32, (rows, LANES), 1)


def merge_kernel(*refs):
    grads, errors, rights = refs[0:3], refs[3:6], refs[6:9]
    merged, partial = refs[9:12], refs[12]
    gbuf, ebuf, rbuf, sems = refs[13:16], refs[16:19], refs[19:22], refs[22]
    copies = []
    index = 0
    for m in range(3):
        for piece in range(COLS[m] // PIECE):
            cols = pl.ds(piece * PIECE, PIECE)
            group = [
                pltpu.make_async_copy(grads[m].at[0, :, cols], gbuf[m].at[:, cols], sems.at[index, 0]),
                pltpu.make_async_copy(errors[m].at[0, :, cols], ebuf[m].at[:, cols], sems.at[index, 1]),
            ]
            if piece == 0:
                group.append(pltpu.make_async_copy(rights[m], rbuf[m], sems.at[index, 2]))
            for copy in group:
                copy.start()
            copies.append((m, piece, group))
            index += 1
    lanes = lane_iota(ROWS)
    result = jnp.zeros((ROWS, LANES), F32)
    totals = None
    for m, piece, group in copies:
        if piece == 0:
            totals = tuple(jnp.zeros((ROWS, LANES), F32) for _ in range(RANK))
        for copy in group:
            copy.wait()

        def step(j, acc, m=m, piece=piece):
            cols = pl.ds(pl.multiple_of(piece * PIECE + j * LANES, LANES), LANES)
            value = gbuf[m][:, cols] + ebuf[m][:, cols].astype(F32)
            merged[m][:, cols] = value
            return tuple(acc[i] + value * rbuf[m][i : i + 1, cols] for i in range(RANK))

        totals = lax.fori_loop(0, PIECE // LANES, step, totals, unroll=8)
        if piece == COLS[m] // PIECE - 1:
            for i in range(RANK):
                column = jnp.sum(totals[i], axis=1, keepdims=True)
                result = jnp.where(lanes == m * RANK + i, column, result)
    for k in range(8):
        partial[k] = result


def sum_replicas(gathered):
    return (
        ((gathered[0] + gathered[1]) + (gathered[2] + gathered[3]))
        + ((gathered[4] + gathered[5]) + (gathered[6] + gathered[7]))
    ) * 0.125


def fold(a, b, distance):
    mask = (lax.broadcasted_iota(jnp.int32, (8, LANES), 0) & distance) == 0
    return jnp.where(mask, a, b) + pltpu.roll(jnp.where(mask, b, a), 8 - distance, 0)


def product_kernel(own, gathered, *refs):
    merged, out = refs[0:3], refs[3]
    core = lax.rem(lax.axis_index("dp"), 2)
    half = core if own else 1 - core
    left = sum_replicas(gathered)
    lanes = lane_iota(1)
    gram = jnp.zeros((1, LANES), F32)
    for shift in range(RANK):
        other = left if shift == 0 else pltpu.roll(left, LANES - shift, 1)
        row = jnp.where(lanes < 3 * RANK, jnp.sum(left * other, axis=0, keepdims=True), 0.0)
        gram = gram + (row if shift == 0 else pltpu.roll(row, 16 * shift, 1))
    for m in range(3):
        columns = [
            jnp.broadcast_to(left[:, m * RANK + i : m * RANK + i + 1], (ROWS, LANES)) for i in range(RANK)
        ]

        def step(block, carry, m=m, columns=columns):
            first = half * (COLS[m] // 2) + block * BLOCK
            row = (FIRST_BLOCK[m] + block) * BLOCK_ROWS
            for pair in range(2):
                terms = []
                for b in range(2):
                    cols = pl.ds(pl.multiple_of(first + (2 * pair + b) * LANES, LANES), LANES)
                    value = merged[m][:, cols]
                    for i in range(RANK):
                        product = columns[i] * value
                        terms.append(product[:8] + product[8:])
                ones = [fold(terms[2 * k], terms[2 * k + 1], 1) for k in range(4)]
                twos = [fold(ones[2 * k], ones[2 * k + 1], 2) for k in range(2)]
                out[pl.ds(row + 8 * pair, 8), :] = fold(twos[0], twos[1], 4)
            out[pl.ds(row + 16, 1), :] = gram
            return carry

        lax.fori_loop(0, HALF_BLOCKS[m], step, 0, unroll=2)


def solve_kernel(blocks, gathered, copies, left_out, scratch):
    total = [jnp.zeros((16, LANES), F32) for _ in range(4)]
    grams = [jnp.zeros((1, LANES), F32) for _ in range(4)]
    for k in range(CHIPS):
        total[k % 4] = total[k % 4] + blocks[k * BLOCK_ROWS : k * BLOCK_ROWS + 16, :]
        grams[k % 4] = grams[k % 4] + blocks[k * BLOCK_ROWS + 16 : k * BLOCK_ROWS + 17, :]
    scratch[...] = (total[0] + total[1]) + (total[2] + total[3])
    gram = ((grams[0] + grams[1]) + (grams[2] + grams[3])) * 0.125

    def entry(i, j):
        shift = 16 * (i - j) + j
        return gram if shift == 0 else pltpu.roll(gram, LANES - shift, 1)

    factor = {}
    for j in range(RANK):
        for i in range(j, RANK):
            value = entry(i, j)
            for k in range(j):
                value = value - factor[i, k] * factor[j, k]
            factor[i, j] = jnp.sqrt(value) if i == j else value / factor[j, j]

    left_sum = sum_replicas(gathered)
    lanes = lane_iota(ROWS)
    valid = (lanes < 3 * RANK) & ((lanes & 3) == 0)
    rows, left = [], jnp.zeros((ROWS, LANES), F32)
    for i in range(RANK):
        current = left_sum if i == 0 else pltpu.roll(left_sum, LANES - i, 1)
        for j in range(i):
            current = current - factor[i, j] * rows[j]
        rows.append(current / factor[i, i])
        kept = jnp.where(valid, rows[i], 0.0)
        left = left + (kept if i == 0 else pltpu.roll(kept, i, 1))
    left_out[...] = left

    mine = (lax.axis_index("dp") // 2) * 16 + lax.axis_index("tensor")
    matrix = jnp.where(mine < FIRST_BLOCK[1], 0, jnp.where(mine < FIRST_BLOCK[2], 1, 2))
    one_lane = lane_iota(1) == matrix * RANK
    nexts = []
    for i in range(RANK):
        current = scratch[pl.ds(i, 4, stride=4), :] * 0.125
        for j in range(i):
            value = jnp.sum(jnp.where(one_lane, factor[i, j], 0.0), axis=1, keepdims=True)
            current = current - value * nexts[j]
        value = jnp.sum(jnp.where(one_lane, factor[i, i], 0.0), axis=1, keepdims=True)
        nexts.append(current / value)
    for i in range(RANK):
        scratch[pl.ds(i, 4, stride=4), :] = nexts[i]
    block = scratch[...]
    for k in range(CHIPS):
        copies[k] = block


OUT_PIECES = (4, 4, 1)


def finish_kernel(own, *refs):
    if own:
        rows, left_ref = refs[0:2]
        merged = refs[2:5]
        nexts, errors, lefts = refs[5:8], refs[8:11], refs[11:14]
        nbuf, ebuf, square, sems = refs[14:17], refs[17:20], refs[20], refs[21]
    else:
        rows, left_ref = refs[0:2]
        merged = refs[2:5]
        nexts, errors = refs[11:14], refs[14:17]
        nbuf, ebuf, sems = refs[17:20], refs[20:23], refs[23]
    core = lax.rem(lax.axis_index("dp"), 2)
    half = core if own else 1 - core
    left = left_ref[...]
    copies = []
    index = 0
    for m in range(3):
        size = COLS[m] // 2 // OUT_PIECES[m]
        columns = [
            jnp.broadcast_to(left[:, m * RANK + i : m * RANK + i + 1], (ROWS, LANES)) for i in range(RANK)
        ]
        for piece in range(OUT_PIECES[m]):

            def step(j, carry, m=m, piece=piece, columns=columns, size=size):
                local = pl.multiple_of(piece * size + j * LANES, LANES)
                value = merged[m][:, pl.ds(pl.multiple_of(half * (COLS[m] // 2) + local, LANES), LANES)]
                row = FIRST_BLOCK[m] * 16 + piece * (size // LANES) * RANK + j * RANK
                nbuf[m][:, pl.ds(local, LANES)] = rows[pl.ds(row, RANK), :]
                approx = columns[0] * rows[pl.ds(row, 1), :]
                for i in range(1, RANK):
                    approx = approx + columns[i] * rows[pl.ds(row + i, 1), :]
                ebuf[m][:, pl.ds(local, LANES)] = (value - approx).astype(BF16)
                return carry

            lax.fori_loop(0, size // LANES, step, 0, unroll=14 if m < 2 else 16)
            here = pl.ds(piece * size, size)
            there = pl.ds(pl.multiple_of(half * (COLS[m] // 2) + piece * size, LANES), size)
            for copy in (
                pltpu.make_async_copy(ebuf[m].at[:, here], errors[m].at[0, :, there], sems.at[index, 0]),
                pltpu.make_async_copy(nbuf[m].at[:, here], nexts[m].at[:, there], sems.at[index, 1]),
            ):
                copy.start()
                copies.append(copy)
            index += 1
    if own:
        square[...] = jnp.zeros((LANES, LANES), F32)
        square[0:ROWS, :] = left
        turned = square[...].T
        for m in range(3):
            lefts[m][...] = turned[m * RANK : (m + 1) * RANK, 0:ROWS]
    for copy in copies:
        copy.wait()


ANY = pl.BlockSpec(memory_space=pl.ANY)
VMEM = pl.BlockSpec(memory_space=pltpu.VMEM)
PARAMS = pltpu.CompilerParams(vmem_limit_bytes=24 * 2**20)


def cost(flops, size):
    return pl.CostEstimate(flops=flops, bytes_accessed=size, transcendentals=0)


def per_device(*args):
    grads, errors, rights = args[0:3], args[3:6], args[6:9]
    pieces = sum(COLS) // PIECE
    grads, errors, rights = ([pltpu.with_memory_space_constraint(x, pltpu.HBM) for x in group] for group in (grads, errors, rights))
    *merged, partial = pl.pallas_call(
        merge_kernel,
        out_shape=[pltpu.VMEM((ROWS, c), F32) for c in COLS] + [jax.ShapeDtypeStruct((8, ROWS, LANES), F32)],
        in_specs=[pl.BlockSpec(memory_space=pltpu.HBM)] * 9,
        out_specs=[VMEM] * 4,
        scratch_shapes=[pltpu.VMEM((ROWS, c), F32) for c in COLS]
        + [pltpu.VMEM((ROWS, c), BF16) for c in COLS]
        + [pltpu.VMEM((RANK, c), F32) for c in COLS]
        + [pltpu.SemaphoreType.DMA((pieces, 3))],
        compiler_params=PARAMS,
        cost_estimate=cost(10**7, 7 * 2**20),
    )(*grads, *errors, *rights)
    gathered = lax.all_to_all(partial, "dp", 0, 0, tiled=True)

    rows = CHIPS * BLOCK_ROWS

    def product(own):
        return pl.pallas_call(
            functools.partial(product_kernel, own),
            out_shape=jax.ShapeDtypeStruct((rows, LANES), F32),
            in_specs=[VMEM] * 4,
            out_specs=VMEM,
            compiler_params=PARAMS,
            cost_estimate=cost(10**7, 5 * 2**20),
        )(gathered, *merged)

    swap = [(i, i ^ 1) for i in range(8)]
    sent = product(False)
    received = lax.ppermute(sent, "dp", swap)
    chip_sum = product(True) + received
    both = ("dp", "tensor")
    chips = [[(2 * x + core) * 16 + t for x in range(4) for t in range(16)] for core in range(2)]
    blocks = lax.all_to_all(
        chip_sum.reshape(CHIPS, 1, BLOCK_ROWS * LANES), both, 0, 0, tiled=True, axis_index_groups=chips
    ).reshape(rows, LANES)

    copies, left = pl.pallas_call(
        solve_kernel,
        out_shape=[
            jax.ShapeDtypeStruct((CHIPS, 16, LANES), F32),
            jax.ShapeDtypeStruct((ROWS, LANES), F32),
        ],
        in_specs=[VMEM] * 2,
        out_specs=[VMEM] * 2,
        scratch_shapes=[pltpu.VMEM((16, LANES), F32)],
        compiler_params=PARAMS,
        cost_estimate=cost(10**6, 2**20),
    )(blocks, gathered)
    mine = lax.all_to_all(copies, both, 0, 0, tiled=True, axis_index_groups=chips).reshape(CHIPS * 16, LANES)
    theirs = lax.ppermute(mine, "dp", swap)

    next_shapes = [jax.ShapeDtypeStruct((RANK, c), F32) for c in COLS]
    error_shapes = [jax.ShapeDtypeStruct((1, ROWS, c), BF16) for c in COLS]
    left_shapes = [jax.ShapeDtypeStruct((RANK, ROWS), F32)] * 3
    scratch = [pltpu.VMEM((RANK, c // 2), F32) for c in COLS] + [pltpu.VMEM((ROWS, c // 2), BF16) for c in COLS]
    sems = pltpu.SemaphoreType.DMA((sum(OUT_PIECES), 2))
    first = pl.pallas_call(
        functools.partial(finish_kernel, True),
        out_shape=next_shapes + error_shapes + left_shapes,
        in_specs=[VMEM] * 5,
        out_specs=[ANY] * 6 + [VMEM] * 3,
        scratch_shapes=scratch + [pltpu.VMEM((LANES, LANES), F32), sems],
        compiler_params=PARAMS,
        cost_estimate=cost(10**7, 4 * 2**20),
    )(mine, left, *merged)
    lefts = first[6:9]
    second = pl.pallas_call(
        functools.partial(finish_kernel, False),
        out_shape=next_shapes + error_shapes,
        in_specs=[VMEM] * 5 + [ANY] * 6,
        out_specs=[ANY] * 6,
        scratch_shapes=scratch + [sems],
        input_output_aliases={5 + k: k for k in range(6)},
        compiler_params=PARAMS,
        cost_estimate=cost(10**7, 4 * 2**20),
    )(theirs, left, *merged, *first[0:6])
    return (*lefts, *second)


def solution(mesh):
    cut = P("dp", "tensor", None)
    return jax.shard_map(
        per_device,
        mesh=mesh,
        in_specs=(cut,) * 6 + (P(),) * 3,
        out_specs=(P(None, "tensor"),) * 3 + (P(),) * 3 + (cut,) * 3,
        check_vma=False,
    )
```

```python
import functools

import jax
import jax.numpy as jnp
from jax import lax
from jax.experimental import pallas as pl
from jax.experimental.pallas import tpu as pltpu
from jax.sharding import PartitionSpec as P

F32 = jnp.float32
BF16 = jnp.bfloat16
RANK = 4
ROWS = 16
LANES = 128
COLS = (28672, 28672, 8192)
BLOCK = 4 * LANES
PIECE = 4096
GROUP = 8
SHARE = 128
SHARE_ROWS = SHARE + 1
HALF_BLOCKS = tuple(c // 2 // BLOCK for c in COLS)
FIRST_BLOCK = (0, HALF_BLOCKS[0], HALF_BLOCKS[0] + HALF_BLOCKS[1])


def lane_iota(rows):
    return lax.broadcasted_iota(jnp.int32, (rows, LANES), 1)


def merge_kernel(*refs):
    grads, errors, rights = refs[0:3], refs[3:6], refs[6:9]
    merged, partial = refs[9:12], refs[12]
    gbuf, ebuf, rbuf, sems = refs[13:16], refs[16:19], refs[19:22], refs[22]
    copies = []
    index = 0
    for m in range(3):
        for piece in range(COLS[m] // PIECE):
            cols = pl.ds(piece * PIECE, PIECE)
            group = [
                pltpu.make_async_copy(grads[m].at[0, :, cols], gbuf[m].at[:, cols], sems.at[index, 0]),
                pltpu.make_async_copy(errors[m].at[0, :, cols], ebuf[m].at[:, cols], sems.at[index, 1]),
            ]
            if piece == 0:
                group.append(pltpu.make_async_copy(rights[m], rbuf[m], sems.at[index, 2]))
            for copy in group:
                copy.start()
            copies.append((m, piece, group))
            index += 1
    lanes = lane_iota(ROWS)
    result = jnp.zeros((ROWS, LANES), F32)
    totals = None
    for m, piece, group in copies:
        if piece == 0:
            totals = tuple(jnp.zeros((ROWS, LANES), F32) for _ in range(RANK))
        for copy in group:
            copy.wait()

        def step(j, acc, m=m, piece=piece):
            cols = pl.ds(pl.multiple_of(piece * PIECE + j * LANES, LANES), LANES)
            value = gbuf[m][:, cols] + ebuf[m][:, cols].astype(F32)
            merged[m][:, cols] = value
            return tuple(acc[i] + value * rbuf[m][i : i + 1, cols] for i in range(RANK))

        totals = lax.fori_loop(0, PIECE // LANES, step, totals, unroll=8)
        if piece == COLS[m] // PIECE - 1:
            for i in range(RANK):
                column = jnp.sum(totals[i], axis=1, keepdims=True)
                result = jnp.where(lanes == m * RANK + i, column, result)
    for k in range(8):
        partial[k] = result


def sum_replicas(gathered):
    return (
        ((gathered[0] + gathered[1]) + (gathered[2] + gathered[3]))
        + ((gathered[4] + gathered[5]) + (gathered[6] + gathered[7]))
    ) * 0.125


def fold(a, b, distance):
    mask = (lax.broadcasted_iota(jnp.int32, (8, LANES), 0) & distance) == 0
    return jnp.where(mask, a, b) + pltpu.roll(jnp.where(mask, b, a), 8 - distance, 0)


def product_kernel(own, gathered, *refs):
    merged, out = refs[0:3], refs[3]
    core = lax.rem(lax.axis_index("dp"), 2)
    half = core if own else 1 - core
    left = sum_replicas(gathered)
    lanes = lane_iota(1)
    gram = jnp.zeros((1, LANES), F32)
    for shift in range(RANK):
        other = left if shift == 0 else pltpu.roll(left, LANES - shift, 1)
        row = jnp.where(lanes < 3 * RANK, jnp.sum(left * other, axis=0, keepdims=True), 0.0)
        gram = gram + (row if shift == 0 else pltpu.roll(row, 16 * shift, 1))
    for m in range(3):
        columns = [
            jnp.broadcast_to(left[:, m * RANK + i : m * RANK + i + 1], (ROWS, LANES)) for i in range(RANK)
        ]

        def step(block, carry, m=m, columns=columns):
            first = half * (COLS[m] // 2) + block * BLOCK
            place = FIRST_BLOCK[m] + block
            row = place * 16 + place // 8
            for pair in range(2):
                terms = []
                for b in range(2):
                    cols = pl.ds(pl.multiple_of(first + (2 * pair + b) * LANES, LANES), LANES)
                    value = merged[m][:, cols]
                    for i in range(RANK):
                        product = columns[i] * value
                        terms.append(product[:8] + product[8:])
                ones = [fold(terms[2 * k], terms[2 * k + 1], 1) for k in range(4)]
                twos = [fold(ones[2 * k], ones[2 * k + 1], 2) for k in range(2)]
                out[pl.ds(row + 8 * pair, 8), :] = fold(twos[0], twos[1], 4)
            return carry

        lax.fori_loop(0, HALF_BLOCKS[m], step, 0, unroll=2)
    for k in range(GROUP):
        out[k * SHARE_ROWS + SHARE : (k + 1) * SHARE_ROWS, :] = gram


def sum_shares(shares, start, rows):
    parts = [shares[k * SHARE_ROWS + start : k * SHARE_ROWS + start + rows, :] for k in range(GROUP)]
    return ((parts[0] + parts[1]) + (parts[2] + parts[3])) + ((parts[4] + parts[5]) + (parts[6] + parts[7]))


def sum_kernel(shares, copies):
    for start in range(0, SHARE_ROWS, 16):
        rows = min(16, SHARE_ROWS - start)
        total = sum_shares(shares, start, rows)
        for k in range(GROUP):
            copies[k * SHARE_ROWS + start : k * SHARE_ROWS + start + rows, :] = total


def solve_kernel(shares, gathered, copies, left_out, scratch):
    for start in range(0, SHARE, 16):
        scratch[start : start + 16, :] = sum_shares(shares, start, 16)
    gram = sum_shares(shares, SHARE, 1) * 0.125

    def entry(i, j):
        shift = 16 * (i - j) + j
        return gram if shift == 0 else pltpu.roll(gram, LANES - shift, 1)

    factor = {}
    for j in range(RANK):
        for i in range(j, RANK):
            value = entry(i, j)
            for k in range(j):
                value = value - factor[i, k] * factor[j, k]
            factor[i, j] = jnp.sqrt(value) if i == j else value / factor[j, j]

    left_sum = sum_replicas(gathered)
    lanes = lane_iota(ROWS)
    valid = (lanes < 3 * RANK) & ((lanes & 3) == 0)
    rows, left = [], jnp.zeros((ROWS, LANES), F32)
    for i in range(RANK):
        current = left_sum if i == 0 else pltpu.roll(left_sum, LANES - i, 1)
        for j in range(i):
            current = current - factor[i, j] * rows[j]
        rows.append(current / factor[i, i])
        kept = jnp.where(valid, rows[i], 0.0)
        left = left + (kept if i == 0 else pltpu.roll(kept, i, 1))
    left_out[...] = left

    dp, tensor = lax.axis_index("dp"), lax.axis_index("tensor")
    place = (dp // 2 % 2) * 4 + (tensor // 4 % 2) * 2 + tensor % 2
    for part in range(2):
        first = (2 * place + part) * (SHARE // 2 // 16)
        matrix = jnp.where(first < FIRST_BLOCK[1], 0, jnp.where(first < FIRST_BLOCK[2], 1, 2))
        one_lane = lane_iota(1) == matrix * RANK
        nexts = []
        for i in range(RANK):
            current = scratch[pl.ds(part * (SHARE // 2) + i, SHARE // 8, stride=RANK), :] * 0.125
            for j in range(i):
                value = jnp.sum(jnp.where(one_lane, factor[i, j], 0.0), axis=1, keepdims=True)
                current = current - value * nexts[j]
            value = jnp.sum(jnp.where(one_lane, factor[i, i], 0.0), axis=1, keepdims=True)
            nexts.append(current / value)
        for i in range(RANK):
            scratch[pl.ds(part * (SHARE // 2) + i, SHARE // 8, stride=RANK), :] = nexts[i]
    for k in range(GROUP):
        copies[k] = scratch[...]


OUT_PIECES = (4, 4, 1)


def finish_kernel(own, *refs):
    if own:
        rows, left_ref = refs[0:2]
        merged = refs[2:5]
        nexts, errors, lefts = refs[5:8], refs[8:11], refs[11:14]
        nbuf, ebuf, square, sems = refs[14:17], refs[17:20], refs[20], refs[21]
    else:
        rows, left_ref = refs[0:2]
        merged = refs[2:5]
        nexts, errors = refs[11:14], refs[14:17]
        nbuf, ebuf, sems = refs[17:20], refs[20:23], refs[23]
    core = lax.rem(lax.axis_index("dp"), 2)
    half = core if own else 1 - core
    left = left_ref[...]
    copies = []
    index = 0
    for m in range(3):
        size = COLS[m] // 2 // OUT_PIECES[m]
        columns = [
            jnp.broadcast_to(left[:, m * RANK + i : m * RANK + i + 1], (ROWS, LANES)) for i in range(RANK)
        ]
        for piece in range(OUT_PIECES[m]):

            def step(j, carry, m=m, piece=piece, columns=columns, size=size):
                local = pl.multiple_of(piece * size + j * LANES, LANES)
                value = merged[m][:, pl.ds(pl.multiple_of(half * (COLS[m] // 2) + local, LANES), LANES)]
                row = FIRST_BLOCK[m] * 16 + piece * (size // LANES) * RANK + j * RANK
                nbuf[m][:, pl.ds(local, LANES)] = rows[pl.ds(row, RANK), :]
                approx = columns[0] * rows[pl.ds(row, 1), :]
                for i in range(1, RANK):
                    approx = approx + columns[i] * rows[pl.ds(row + i, 1), :]
                ebuf[m][:, pl.ds(local, LANES)] = (value - approx).astype(BF16)
                return carry

            lax.fori_loop(0, size // LANES, step, 0, unroll=14 if m < 2 else 16)
            here = pl.ds(piece * size, size)
            there = pl.ds(pl.multiple_of(half * (COLS[m] // 2) + piece * size, LANES), size)
            for copy in (
                pltpu.make_async_copy(ebuf[m].at[:, here], errors[m].at[0, :, there], sems.at[index, 0]),
                pltpu.make_async_copy(nbuf[m].at[:, here], nexts[m].at[:, there], sems.at[index, 1]),
            ):
                copy.start()
                copies.append(copy)
            index += 1
    if own:
        square[...] = jnp.zeros((LANES, LANES), F32)
        square[0:ROWS, :] = left
        turned = square[...].T
        for m in range(3):
            lefts[m][...] = turned[m * RANK : (m + 1) * RANK, 0:ROWS]
    for copy in copies:
        copy.wait()


ANY = pl.BlockSpec(memory_space=pl.ANY)
VMEM = pl.BlockSpec(memory_space=pltpu.VMEM)
PARAMS = pltpu.CompilerParams(vmem_limit_bytes=24 * 2**20)


def cost(flops, size):
    return pl.CostEstimate(flops=flops, bytes_accessed=size, transcendentals=0)


def groups():
    at = {}
    for x in range(4):
        for core in range(2):
            for z in range(4):
                for y in range(4):
                    place = (x % 2) * 4 + (z % 2) * 2 + y % 2
                    cube = (x // 2) * 4 + (z // 2) * 2 + y // 2
                    at[core, cube, place] = (2 * x + core) * 16 + z * 4 + y
    cubes = [[at[core, cube, place] for place in range(8)] for core in range(2) for cube in range(8)]
    peers = [[at[core, cube, place] for cube in range(8)] for core in range(2) for place in range(8)]
    return cubes, peers


def per_device(*args):
    grads, errors, rights = args[0:3], args[3:6], args[6:9]
    pieces = sum(COLS) // PIECE
    grads, errors, rights = ([pltpu.with_memory_space_constraint(x, pltpu.HBM) for x in group] for group in (grads, errors, rights))
    *merged, partial = pl.pallas_call(
        merge_kernel,
        out_shape=[pltpu.VMEM((ROWS, c), F32) for c in COLS] + [jax.ShapeDtypeStruct((8, ROWS, LANES), F32)],
        in_specs=[pl.BlockSpec(memory_space=pltpu.HBM)] * 9,
        out_specs=[VMEM] * 4,
        scratch_shapes=[pltpu.VMEM((ROWS, c), F32) for c in COLS]
        + [pltpu.VMEM((ROWS, c), BF16) for c in COLS]
        + [pltpu.VMEM((RANK, c), F32) for c in COLS]
        + [pltpu.SemaphoreType.DMA((pieces, 3))],
        compiler_params=PARAMS,
        cost_estimate=cost(10**7, 7 * 2**20),
    )(*grads, *errors, *rights)
    gathered = lax.all_to_all(partial, "dp", 0, 0, tiled=True)

    rows = GROUP * SHARE_ROWS
    both = ("dp", "tensor")
    cubes, peers = groups()

    def exchange(shares, members):
        flat = shares.reshape(GROUP, 1, SHARE_ROWS * LANES)
        return lax.all_to_all(flat, both, 0, 0, tiled=True, axis_index_groups=members).reshape(rows, LANES)

    def product(own):
        return pl.pallas_call(
            functools.partial(product_kernel, own),
            out_shape=jax.ShapeDtypeStruct((rows, LANES), F32),
            in_specs=[VMEM] * 4,
            out_specs=VMEM,
            compiler_params=PARAMS,
            cost_estimate=cost(10**7, 5 * 2**20),
        )(gathered, *merged)

    swap = [(i, i ^ 1) for i in range(8)]
    sent = product(False)
    received = lax.ppermute(sent, "dp", swap)
    chip_sum = product(True) + received
    cube_sums = pl.pallas_call(
        sum_kernel,
        out_shape=jax.ShapeDtypeStruct((rows, LANES), F32),
        in_specs=[VMEM],
        out_specs=VMEM,
        compiler_params=PARAMS,
        cost_estimate=cost(10**5, 2**20),
    )(exchange(chip_sum, cubes))
    copies, left = pl.pallas_call(
        solve_kernel,
        out_shape=[
            jax.ShapeDtypeStruct((GROUP, SHARE, LANES), F32),
            jax.ShapeDtypeStruct((ROWS, LANES), F32),
        ],
        in_specs=[VMEM] * 2,
        out_specs=[VMEM] * 2,
        scratch_shapes=[pltpu.VMEM((SHARE, LANES), F32)],
        compiler_params=PARAMS,
        cost_estimate=cost(10**6, 2**20),
    )(exchange(cube_sums, peers), gathered)
    mine = lax.all_to_all(copies, both, 0, 0, tiled=True, axis_index_groups=cubes).reshape(GROUP * SHARE, LANES)
    theirs = lax.ppermute(mine, "dp", swap)

    next_shapes = [jax.ShapeDtypeStruct((RANK, c), F32) for c in COLS]
    error_shapes = [jax.ShapeDtypeStruct((1, ROWS, c), BF16) for c in COLS]
    left_shapes = [jax.ShapeDtypeStruct((RANK, ROWS), F32)] * 3
    scratch = [pltpu.VMEM((RANK, c // 2), F32) for c in COLS] + [pltpu.VMEM((ROWS, c // 2), BF16) for c in COLS]
    sems = pltpu.SemaphoreType.DMA((sum(OUT_PIECES), 2))
    first = pl.pallas_call(
        functools.partial(finish_kernel, True),
        out_shape=next_shapes + error_shapes + left_shapes,
        in_specs=[VMEM] * 5,
        out_specs=[ANY] * 6 + [VMEM] * 3,
        scratch_shapes=scratch + [pltpu.VMEM((LANES, LANES), F32), sems],
        compiler_params=PARAMS,
        cost_estimate=cost(10**7, 4 * 2**20),
    )(mine, left, *merged)
    lefts = first[6:9]
    second = pl.pallas_call(
        functools.partial(finish_kernel, False),
        out_shape=next_shapes + error_shapes,
        in_specs=[VMEM] * 5 + [ANY] * 6,
        out_specs=[ANY] * 6,
        scratch_shapes=scratch + [sems],
        input_output_aliases={5 + k: k for k in range(6)},
        compiler_params=PARAMS,
        cost_estimate=cost(10**7, 4 * 2**20),
    )(theirs, left, *merged, *first[0:6])
    return (*lefts, *second)


def solution(mesh):
    cut = P("dp", "tensor", None)
    return jax.shard_map(
        per_device,
        mesh=mesh,
        in_specs=(cut,) * 6 + (P(),) * 3,
        out_specs=(P(None, "tensor"),) * 3 + (P(),) * 3 + (cut,) * 3,
        check_vma=False,
    )
```

```python
import functools

import jax
import jax.numpy as jnp
from jax import lax
from jax.experimental import pallas as pl
from jax.experimental.pallas import tpu as pltpu
from jax.sharding import PartitionSpec as P

F32 = jnp.float32
BF16 = jnp.bfloat16
RANK = 4
ROWS = 16
LANES = 128
COLS = (28672, 28672, 8192)
BLOCK = 4 * LANES
OTHER_PIECES = ((0, 2048), (0, 4096), (0, 8192), (1, 14336), (2, 4096))
OWN_PIECES = ((2, 4096), (0, 14336), (1, 8192), (1, 4096), (1, 2048))
CHIPS = 64
BLOCK_ROWS = 17
HALF_BLOCKS = tuple(c // 2 // BLOCK for c in COLS)
FIRST_BLOCK = (0, HALF_BLOCKS[0], HALF_BLOCKS[0] + HALF_BLOCKS[1])
HALF = sum(COLS) // 2


def lane_iota(rows):
    return lax.broadcasted_iota(jnp.int32, (rows, LANES), 1)


def merge_kernel(*refs):
    grads, errors, rights = refs[0:3], refs[3:6], refs[6:9]
    merged, sent, partial = refs[9:12], refs[12], refs[13]
    gbuf, ebuf, rbuf, sems = refs[14:17], refs[17:20], refs[20:23], refs[23]
    core = lax.rem(lax.axis_index("dp"), 2)
    copies, begun = [], set()
    for own, pieces in ((False, OTHER_PIECES), (True, OWN_PIECES)):
        done = [0, 0, 0]
        for m, size in pieces:
            half = core if own else 1 - core
            start = pl.multiple_of(half * (COLS[m] // 2) + done[m], LANES)
            cols = pl.ds(start, size)
            index = len(copies)
            group = []
            if m not in begun:
                begun.add(m)
                group.append(pltpu.make_async_copy(rights[m], rbuf[m], sems.at[index, 2]))
            group.append(pltpu.make_async_copy(grads[m].at[0, :, cols], gbuf[m].at[:, cols], sems.at[index, 0]))
            group.append(pltpu.make_async_copy(errors[m].at[0, :, cols], ebuf[m].at[:, cols], sems.at[index, 1]))
            for copy in group:
                copy.start()
            copies.append((own, m, start, FIRST_BLOCK[m] * BLOCK + done[m], size, group))
            done[m] += size
    totals = [tuple(jnp.zeros((ROWS, LANES), F32) for _ in range(RANK)) for _ in range(3)]
    for own, m, start, place, size, group in copies:
        for copy in group:
            copy.wait()

        def step(j, acc, own=own, m=m, start=start, place=place):
            cols = pl.ds(pl.multiple_of(start + j * LANES, LANES), LANES)
            value = gbuf[m][:, cols] + ebuf[m][:, cols].astype(F32)
            merged[m][:, cols] = value
            if not own:
                sent[:, pl.ds(pl.multiple_of(place + j * LANES, LANES), LANES)] = value
            return tuple(acc[i] + value * rbuf[m][i : i + 1, cols] for i in range(RANK))

        totals[m] = lax.fori_loop(0, size // LANES, step, totals[m], unroll=16)
    lanes = lane_iota(ROWS)
    result = jnp.zeros((ROWS, LANES), F32)
    for m in range(3):
        for i in range(RANK):
            column = jnp.sum(totals[m][i], axis=1, keepdims=True)
            result = jnp.where(lanes == m * RANK + i, column, result)
    for k in range(8):
        partial[k] = result


def sum_replicas(gathered):
    return (
        ((gathered[0] + gathered[1]) + (gathered[2] + gathered[3]))
        + ((gathered[4] + gathered[5]) + (gathered[6] + gathered[7]))
    ) * 0.125


def fold(a, b, distance):
    mask = (lax.broadcasted_iota(jnp.int32, (8, LANES), 0) & distance) == 0
    return jnp.where(mask, a, b) + pltpu.roll(jnp.where(mask, b, a), 8 - distance, 0)


def product_kernel(gathered, received, *refs):
    merged, out = refs[0:3], refs[3]
    core = lax.rem(lax.axis_index("dp"), 2)
    left = sum_replicas(gathered)
    lanes = lane_iota(1)
    gram = jnp.zeros((1, LANES), F32)
    for shift in range(RANK):
        other = left if shift == 0 else pltpu.roll(left, LANES - shift, 1)
        row = jnp.where(lanes < 3 * RANK, jnp.sum(left * other, axis=0, keepdims=True), 0.0)
        gram = gram + (row if shift == 0 else pltpu.roll(row, 16 * shift, 1))
    for m in range(3):
        columns = [
            jnp.broadcast_to(left[:, m * RANK + i : m * RANK + i + 1], (ROWS, LANES)) for i in range(RANK)
        ]

        def step(block, carry, m=m, columns=columns):
            first = core * (COLS[m] // 2) + block * BLOCK
            place = (FIRST_BLOCK[m] + block) * BLOCK
            row = (FIRST_BLOCK[m] + block) * BLOCK_ROWS
            for pair in range(2):
                terms = []
                for b in range(2):
                    shift = (2 * pair + b) * LANES
                    mine = merged[m][:, pl.ds(pl.multiple_of(first + shift, LANES), LANES)]
                    value = mine + received[:, pl.ds(pl.multiple_of(place + shift, LANES), LANES)]
                    for i in range(RANK):
                        product = columns[i] * value
                        terms.append(product[:8] + product[8:])
                ones = [fold(terms[2 * k], terms[2 * k + 1], 1) for k in range(4)]
                twos = [fold(ones[2 * k], ones[2 * k + 1], 2) for k in range(2)]
                out[pl.ds(row + 8 * pair, 8), :] = fold(twos[0], twos[1], 4)
            out[pl.ds(row + 16, 1), :] = gram
            return carry

        lax.fori_loop(0, HALF_BLOCKS[m], step, 0, unroll=4)


def solve_kernel(blocks, gathered, copies, left_out, scratch):
    total = [jnp.zeros((16, LANES), F32) for _ in range(4)]
    grams = [jnp.zeros((1, LANES), F32) for _ in range(4)]
    for k in range(CHIPS):
        total[k % 4] = total[k % 4] + blocks[k * BLOCK_ROWS : k * BLOCK_ROWS + 16, :]
        grams[k % 4] = grams[k % 4] + blocks[k * BLOCK_ROWS + 16 : k * BLOCK_ROWS + 17, :]
    scratch[...] = (total[0] + total[1]) + (total[2] + total[3])
    gram = ((grams[0] + grams[1]) + (grams[2] + grams[3])) * 0.25

    def entry(i, j):
        shift = 16 * (i - j) + j
        return gram if shift == 0 else pltpu.roll(gram, LANES - shift, 1)

    factor = {}
    for j in range(RANK):
        for i in range(j, RANK):
            value = entry(i, j)
            for k in range(j):
                value = value - factor[i, k] * factor[j, k]
            factor[i, j] = jnp.sqrt(value) if i == j else value / factor[j, j]

    left_sum = sum_replicas(gathered)
    lanes = lane_iota(ROWS)
    valid = (lanes < 3 * RANK) & ((lanes & 3) == 0)
    rows, left = [], jnp.zeros((ROWS, LANES), F32)
    for i in range(RANK):
        current = left_sum if i == 0 else pltpu.roll(left_sum, LANES - i, 1)
        for j in range(i):
            current = current - factor[i, j] * rows[j]
        rows.append(current / factor[i, i])
        kept = jnp.where(valid, rows[i], 0.0)
        left = left + (kept if i == 0 else pltpu.roll(kept, i, 1))
    left_out[...] = left

    mine = (lax.axis_index("dp") // 2) * 16 + lax.axis_index("tensor")
    matrix = jnp.where(mine < FIRST_BLOCK[1], 0, jnp.where(mine < FIRST_BLOCK[2], 1, 2))
    one_lane = lane_iota(1) == matrix * RANK
    nexts = []
    for i in range(RANK):
        current = scratch[pl.ds(i, 4, stride=4), :] * 0.125
        for j in range(i):
            value = jnp.sum(jnp.where(one_lane, factor[i, j], 0.0), axis=1, keepdims=True)
            current = current - value * nexts[j]
        value = jnp.sum(jnp.where(one_lane, factor[i, i], 0.0), axis=1, keepdims=True)
        nexts.append(current / value)
    for i in range(RANK):
        scratch[pl.ds(i, 4, stride=4), :] = nexts[i]
    block = scratch[...]
    for k in range(CHIPS):
        copies[k] = block


OUT_PIECES = (4, 4, 1)


def finish_kernel(own, *refs):
    if own:
        rows, left_ref = refs[0:2]
        merged = refs[2:5]
        nexts, errors, lefts = refs[5:8], refs[8:11], refs[11:14]
        nbuf, ebuf, square, sems = refs[14:17], refs[17:20], refs[20], refs[21]
    else:
        rows, left_ref = refs[0:2]
        merged = refs[2:5]
        nexts, errors = refs[11:14], refs[14:17]
        nbuf, ebuf, sems = refs[17:20], refs[20:23], refs[23]
    core = lax.rem(lax.axis_index("dp"), 2)
    half = core if own else 1 - core
    left = left_ref[...]
    copies = []
    index = 0
    for m in range(3):
        size = COLS[m] // 2 // OUT_PIECES[m]
        columns = [
            jnp.broadcast_to(left[:, m * RANK + i : m * RANK + i + 1], (ROWS, LANES)) for i in range(RANK)
        ]
        for piece in range(OUT_PIECES[m]):

            def step(j, carry, m=m, piece=piece, columns=columns, size=size):
                local = pl.multiple_of(piece * size + j * LANES, LANES)
                value = merged[m][:, pl.ds(pl.multiple_of(half * (COLS[m] // 2) + local, LANES), LANES)]
                row = FIRST_BLOCK[m] * 16 + piece * (size // LANES) * RANK + j * RANK
                nbuf[m][:, pl.ds(local, LANES)] = rows[pl.ds(row, RANK), :]
                approx = columns[0] * rows[pl.ds(row, 1), :]
                for i in range(1, RANK):
                    approx = approx + columns[i] * rows[pl.ds(row + i, 1), :]
                ebuf[m][:, pl.ds(local, LANES)] = (value - approx).astype(BF16)
                return carry

            lax.fori_loop(0, size // LANES, step, 0, unroll=14 if m < 2 else 16)
            here = pl.ds(piece * size, size)
            there = pl.ds(pl.multiple_of(half * (COLS[m] // 2) + piece * size, LANES), size)
            for copy in (
                pltpu.make_async_copy(ebuf[m].at[:, here], errors[m].at[0, :, there], sems.at[index, 0]),
                pltpu.make_async_copy(nbuf[m].at[:, here], nexts[m].at[:, there], sems.at[index, 1]),
            ):
                copy.start()
                copies.append(copy)
            index += 1
    if own:
        square[...] = jnp.zeros((LANES, LANES), F32)
        square[0:ROWS, :] = left
        turned = square[...].T
        for m in range(3):
            lefts[m][...] = turned[m * RANK : (m + 1) * RANK, 0:ROWS]
    for copy in copies:
        copy.wait()


ANY = pl.BlockSpec(memory_space=pl.ANY)
VMEM = pl.BlockSpec(memory_space=pltpu.VMEM)
PARAMS = pltpu.CompilerParams(vmem_limit_bytes=24 * 2**20)


def cost(flops, size):
    return pl.CostEstimate(flops=flops, bytes_accessed=size, transcendentals=0)


def per_device(*args):
    grads, errors, rights = args[0:3], args[3:6], args[6:9]
    grads, errors, rights = (
        [pltpu.with_memory_space_constraint(x, pltpu.HBM) for x in group] for group in (grads, errors, rights)
    )
    *merged, sent, partial = pl.pallas_call(
        merge_kernel,
        out_shape=[pltpu.VMEM((ROWS, c), F32) for c in COLS]
        + [jax.ShapeDtypeStruct((ROWS, HALF), F32), jax.ShapeDtypeStruct((8, ROWS, LANES), F32)],
        in_specs=[pl.BlockSpec(memory_space=pltpu.HBM)] * 9,
        out_specs=[VMEM] * 5,
        scratch_shapes=[pltpu.VMEM((ROWS, c), F32) for c in COLS]
        + [pltpu.VMEM((ROWS, c), BF16) for c in COLS]
        + [pltpu.VMEM((RANK, c), F32) for c in COLS]
        + [pltpu.SemaphoreType.DMA((len(OTHER_PIECES + OWN_PIECES), 3))],
        compiler_params=PARAMS,
        cost_estimate=cost(10**7, 7 * 2**20),
    )(*grads, *errors, *rights)
    swap = [(i, i ^ 1) for i in range(8)]
    received = lax.ppermute(sent, "dp", swap)
    gathered = lax.all_to_all(partial, "dp", 0, 0, tiled=True)

    rows = CHIPS * BLOCK_ROWS
    chip_sum = pl.pallas_call(
        product_kernel,
        out_shape=jax.ShapeDtypeStruct((rows, LANES), F32),
        in_specs=[VMEM] * 5,
        out_specs=VMEM,
        compiler_params=PARAMS,
        cost_estimate=cost(10**7, 5 * 2**20),
    )(gathered, received, *merged)
    both = ("dp", "tensor")
    chips = [[(2 * x + core) * 16 + t for x in range(4) for t in range(16)] for core in range(2)]
    blocks = lax.all_to_all(
        chip_sum.reshape(CHIPS, 1, BLOCK_ROWS * LANES), both, 0, 0, tiled=True, axis_index_groups=chips
    ).reshape(rows, LANES)

    copies, left = pl.pallas_call(
        solve_kernel,
        out_shape=[
            jax.ShapeDtypeStruct((CHIPS, 16, LANES), F32),
            jax.ShapeDtypeStruct((ROWS, LANES), F32),
        ],
        in_specs=[VMEM] * 2,
        out_specs=[VMEM] * 2,
        scratch_shapes=[pltpu.VMEM((16, LANES), F32)],
        compiler_params=PARAMS,
        cost_estimate=cost(10**6, 2**20),
    )(blocks, gathered)
    mine = lax.all_to_all(copies, both, 0, 0, tiled=True, axis_index_groups=chips).reshape(CHIPS * 16, LANES)
    theirs = lax.ppermute(mine, "dp", swap)

    next_shapes = [jax.ShapeDtypeStruct((RANK, c), F32) for c in COLS]
    error_shapes = [jax.ShapeDtypeStruct((1, ROWS, c), BF16) for c in COLS]
    left_shapes = [jax.ShapeDtypeStruct((RANK, ROWS), F32)] * 3
    scratch = [pltpu.VMEM((RANK, c // 2), F32) for c in COLS] + [pltpu.VMEM((ROWS, c // 2), BF16) for c in COLS]
    sems = pltpu.SemaphoreType.DMA((sum(OUT_PIECES), 2))
    first = pl.pallas_call(
        functools.partial(finish_kernel, True),
        out_shape=next_shapes + error_shapes + left_shapes,
        in_specs=[VMEM] * 5,
        out_specs=[ANY] * 6 + [VMEM] * 3,
        scratch_shapes=scratch + [pltpu.VMEM((LANES, LANES), F32), sems],
        compiler_params=PARAMS,
        cost_estimate=cost(10**7, 4 * 2**20),
    )(mine, left, *merged)
    lefts = first[6:9]
    second = pl.pallas_call(
        functools.partial(finish_kernel, False),
        out_shape=next_shapes + error_shapes,
        in_specs=[VMEM] * 5 + [ANY] * 6,
        out_specs=[ANY] * 6,
        scratch_shapes=scratch + [sems],
        input_output_aliases={5 + k: k for k in range(6)},
        compiler_params=PARAMS,
        cost_estimate=cost(10**7, 4 * 2**20),
    )(theirs, left, *merged, *first[0:6])
    return (*lefts, *second)


def solution(mesh):
    cut = P("dp", "tensor", None)
    return jax.shard_map(
        per_device,
        mesh=mesh,
        in_specs=(cut,) * 6 + (P(),) * 3,
        out_specs=(P(None, "tensor"),) * 3 + (P(),) * 3 + (cut,) * 3,
        check_vma=False,
    )
```

```python
import functools

import jax
import jax.numpy as jnp
from jax import lax
from jax.experimental import pallas as pl
from jax.experimental.pallas import tpu as pltpu
from jax.sharding import PartitionSpec as P

F32 = jnp.float32
BF16 = jnp.bfloat16
RANK = 4
ROWS = 16
LANES = 128
COLS = (28672, 28672, 8192)
BLOCK = 4 * LANES
OTHER_PIECES = ((0, 4096), (0, 10240), (1, 14336), (2, 4096))
OWN_PIECES = ((0, 14336), (2, 4096), (1, 10240), (1, 4096))
CHIPS = 64
BLOCK_ROWS = 17
HALF_BLOCKS = tuple(c // 2 // BLOCK for c in COLS)
FIRST_BLOCK = (0, HALF_BLOCKS[0], HALF_BLOCKS[0] + HALF_BLOCKS[1])
HALF = sum(COLS) // 2


def lane_iota(rows):
    return lax.broadcasted_iota(jnp.int32, (rows, LANES), 1)


def merge_kernel(*refs):
    grads, errors, rights = refs[0:3], refs[3:6], refs[6:9]
    merged, sent, partial = refs[9:12], refs[12], refs[13]
    gbuf, ebuf, rbuf, sems = refs[14:17], refs[17:20], refs[20:23], refs[23]
    core = lax.rem(lax.axis_index("dp"), 2)
    copies = []
    for own, pieces in ((False, OTHER_PIECES), (True, OWN_PIECES)):
        done = [0, 0, 0]
        for m, size in pieces:
            half = core if own else 1 - core
            start = pl.multiple_of(half * (COLS[m] // 2) + done[m], LANES)
            cols = pl.ds(start, size)
            index = len(copies)
            group = []
            if done[m] == 0:
                whole = pl.ds(start, COLS[m] // 2)
                group.append(pltpu.make_async_copy(rights[m].at[:, whole], rbuf[m].at[:, whole], sems.at[index, 2]))
            group.append(pltpu.make_async_copy(grads[m].at[0, :, cols], gbuf[m].at[:, cols], sems.at[index, 0]))
            group.append(pltpu.make_async_copy(errors[m].at[0, :, cols], ebuf[m].at[:, cols], sems.at[index, 1]))
            for copy in group:
                copy.start()
            copies.append((own, m, start, FIRST_BLOCK[m] * BLOCK + done[m], size, group))
            done[m] += size
    totals = [tuple(jnp.zeros((ROWS, LANES), F32) for _ in range(RANK)) for _ in range(3)]
    for own, m, start, place, size, group in copies:
        for copy in group:
            copy.wait()

        def step(j, acc, own=own, m=m, start=start, place=place):
            cols = pl.ds(pl.multiple_of(start + j * LANES, LANES), LANES)
            value = gbuf[m][:, cols] + ebuf[m][:, cols].astype(F32)
            merged[m][:, cols] = value
            if not own:
                sent[:, pl.ds(pl.multiple_of(place + j * LANES, LANES), LANES)] = value
            return tuple(acc[i] + value * rbuf[m][i : i + 1, cols] for i in range(RANK))

        totals[m] = lax.fori_loop(0, size // LANES, step, totals[m], unroll=16)
    lanes = lane_iota(ROWS)
    result = jnp.zeros((ROWS, LANES), F32)
    for m in range(3):
        for i in range(RANK):
            column = jnp.sum(totals[m][i], axis=1, keepdims=True)
            result = jnp.where(lanes == m * RANK + i, column, result)
    partial[...] = result


def sum_replicas(parts):
    return ((parts[0][...] + parts[2][...]) + (parts[1][...] + parts[3][...])) * 0.125


def fold(a, b, distance):
    mask = (lax.broadcasted_iota(jnp.int32, (8, LANES), 0) & distance) == 0
    return jnp.where(mask, a, b) + pltpu.roll(jnp.where(mask, b, a), 8 - distance, 0)


def product_kernel(*refs):
    gathered, received, merged, out = refs[0:4], refs[4], refs[5:8], refs[8]
    core = lax.rem(lax.axis_index("dp"), 2)
    left = sum_replicas(gathered)
    lanes = lane_iota(1)
    gram = jnp.zeros((1, LANES), F32)
    for shift in range(RANK):
        other = left if shift == 0 else pltpu.roll(left, LANES - shift, 1)
        row = jnp.where(lanes < 3 * RANK, jnp.sum(left * other, axis=0, keepdims=True), 0.0)
        gram = gram + (row if shift == 0 else pltpu.roll(row, 16 * shift, 1))
    for m in range(3):
        columns = [
            jnp.broadcast_to(left[:, m * RANK + i : m * RANK + i + 1], (ROWS, LANES)) for i in range(RANK)
        ]

        def step(block, carry, m=m, columns=columns):
            first = core * (COLS[m] // 2) + block * BLOCK
            place = (FIRST_BLOCK[m] + block) * BLOCK
            row = (FIRST_BLOCK[m] + block) * BLOCK_ROWS
            for pair in range(2):
                terms = []
                for b in range(2):
                    shift = (2 * pair + b) * LANES
                    mine = merged[m][:, pl.ds(pl.multiple_of(first + shift, LANES), LANES)]
                    value = mine + received[:, pl.ds(pl.multiple_of(place + shift, LANES), LANES)]
                    for i in range(RANK):
                        product = columns[i] * value
                        terms.append(product[:8] + product[8:])
                ones = [fold(terms[2 * k], terms[2 * k + 1], 1) for k in range(4)]
                twos = [fold(ones[2 * k], ones[2 * k + 1], 2) for k in range(2)]
                out[pl.ds(row + 8 * pair, 8), :] = fold(twos[0], twos[1], 4)
            out[pl.ds(row + 16, 1), :] = gram
            return carry

        lax.fori_loop(0, HALF_BLOCKS[m], step, 0, unroll=4)


def solve_kernel(blocks, *refs):
    gathered, copies, left_out, scratch = refs[0:4], refs[4], refs[5], refs[6]
    total = [jnp.zeros((16, LANES), F32) for _ in range(4)]
    grams = [jnp.zeros((1, LANES), F32) for _ in range(4)]
    for k in range(CHIPS):
        total[k % 4] = total[k % 4] + blocks[k * BLOCK_ROWS : k * BLOCK_ROWS + 16, :]
        grams[k % 4] = grams[k % 4] + blocks[k * BLOCK_ROWS + 16 : k * BLOCK_ROWS + 17, :]
    scratch[...] = (total[0] + total[1]) + (total[2] + total[3])
    gram = ((grams[0] + grams[1]) + (grams[2] + grams[3])) * 0.25

    def entry(i, j):
        shift = 16 * (i - j) + j
        return gram if shift == 0 else pltpu.roll(gram, LANES - shift, 1)

    factor = {}
    for j in range(RANK):
        for i in range(j, RANK):
            value = entry(i, j)
            for k in range(j):
                value = value - factor[i, k] * factor[j, k]
            factor[i, j] = jnp.sqrt(value) if i == j else value / factor[j, j]

    left_sum = sum_replicas(gathered)
    lanes = lane_iota(ROWS)
    valid = (lanes < 3 * RANK) & ((lanes & 3) == 0)
    rows, left = [], jnp.zeros((ROWS, LANES), F32)
    for i in range(RANK):
        current = left_sum if i == 0 else pltpu.roll(left_sum, LANES - i, 1)
        for j in range(i):
            current = current - factor[i, j] * rows[j]
        rows.append(current / factor[i, i])
        kept = jnp.where(valid, rows[i], 0.0)
        left = left + (kept if i == 0 else pltpu.roll(kept, i, 1))
    left_out[...] = left

    mine = CHIPS - 1 - ((lax.axis_index("dp") // 2) * 16 + lax.axis_index("tensor"))
    matrix = jnp.where(mine < FIRST_BLOCK[1], 0, jnp.where(mine < FIRST_BLOCK[2], 1, 2))
    one_lane = lane_iota(1) == matrix * RANK
    nexts = []
    for i in range(RANK):
        current = scratch[pl.ds(i, 4, stride=4), :] * 0.125
        for j in range(i):
            value = jnp.sum(jnp.where(one_lane, factor[i, j], 0.0), axis=1, keepdims=True)
            current = current - value * nexts[j]
        value = jnp.sum(jnp.where(one_lane, factor[i, i], 0.0), axis=1, keepdims=True)
        nexts.append(current / value)
    for i in range(RANK):
        scratch[pl.ds(i, 4, stride=4), :] = nexts[i]
    block = scratch[...]
    for k in range(CHIPS):
        copies[16 * k : 16 * k + 16, :] = block


OUT_PIECES = (4, 4, 1)


def finish_kernel(own, *refs):
    rows, left_ref, merged = refs[0], refs[1], refs[2:5]
    if own:
        nexts, errors, lefts = refs[5:8], refs[8:11], refs[11:14]
        nbuf, ebuf, sems, square, lbuf, lsems = refs[14:17], refs[17:20], refs[20], refs[21], refs[22:25], refs[25]
    else:
        nexts, errors = refs[11:14], refs[14:17]
        nbuf, ebuf, sems = refs[17:20], refs[20:23], refs[23]
    core = lax.rem(lax.axis_index("dp"), 2)
    half = core if own else 1 - core
    left = left_ref[...]
    copies = []
    if own:
        square[...] = jnp.zeros((LANES, LANES), F32)
        square[0:ROWS, :] = left
        turned = square[...].T
        for m in range(3):
            lbuf[m][...] = turned[m * RANK : (m + 1) * RANK, 0:ROWS]
            copy = pltpu.make_async_copy(lbuf[m], lefts[m], lsems.at[m])
            copy.start()
            copies.append(copy)
    index = 0
    for m in range(3):
        size = COLS[m] // 2 // OUT_PIECES[m]
        columns = [
            jnp.broadcast_to(left[:, m * RANK + i : m * RANK + i + 1], (ROWS, LANES)) for i in range(RANK)
        ]
        for piece in range(OUT_PIECES[m]):

            def step(j, carry, m=m, piece=piece, columns=columns, size=size):
                local = pl.multiple_of(piece * size + j * LANES, LANES)
                value = merged[m][:, pl.ds(pl.multiple_of(half * (COLS[m] // 2) + local, LANES), LANES)]
                row = FIRST_BLOCK[m] * 16 + piece * (size // LANES) * RANK + j * RANK
                nbuf[m][:, pl.ds(local, LANES)] = rows[pl.ds(row, RANK), :]
                approx = columns[0] * rows[pl.ds(row, 1), :]
                for i in range(1, RANK):
                    approx = approx + columns[i] * rows[pl.ds(row + i, 1), :]
                ebuf[m][:, pl.ds(local, LANES)] = (value - approx).astype(BF16)
                return carry

            lax.fori_loop(0, size // LANES, step, 0, unroll=14 if m < 2 else 16)
            here = pl.ds(piece * size, size)
            there = pl.ds(pl.multiple_of(half * (COLS[m] // 2) + piece * size, LANES), size)
            for copy in (
                pltpu.make_async_copy(ebuf[m].at[:, here], errors[m].at[0, :, there], sems.at[index, 0]),
                pltpu.make_async_copy(nbuf[m].at[:, here], nexts[m].at[:, there], sems.at[index, 1]),
            ):
                copy.start()
                copies.append(copy)
            index += 1
    for copy in copies:
        copy.wait()


ANY = pl.BlockSpec(memory_space=pl.ANY)
VMEM = pl.BlockSpec(memory_space=pltpu.VMEM)
PARAMS = pltpu.CompilerParams(vmem_limit_bytes=24 * 2**20)


def cost(flops, size):
    return pl.CostEstimate(flops=flops, bytes_accessed=size, transcendentals=0)


def per_device(*args):
    grads, errors, rights = args[0:3], args[3:6], args[6:9]
    grads, errors, rights = (
        [pltpu.with_memory_space_constraint(x, pltpu.HBM) for x in group] for group in (grads, errors, rights)
    )
    *merged, sent, partial = pl.pallas_call(
        merge_kernel,
        out_shape=[pltpu.VMEM((ROWS, c), F32) for c in COLS]
        + [jax.ShapeDtypeStruct((ROWS, HALF), F32), jax.ShapeDtypeStruct((ROWS, LANES), F32)],
        in_specs=[pl.BlockSpec(memory_space=pltpu.HBM)] * 9,
        out_specs=[VMEM] * 5,
        scratch_shapes=[pltpu.VMEM((ROWS, c), F32) for c in COLS]
        + [pltpu.VMEM((ROWS, c), BF16) for c in COLS]
        + [pltpu.VMEM((RANK, c), F32) for c in COLS]
        + [pltpu.SemaphoreType.DMA((len(OTHER_PIECES + OWN_PIECES), 3))],
        compiler_params=PARAMS,
        cost_estimate=cost(10**7, 7 * 2**20),
    )(*grads, *errors, *rights)
    swap = [(i, i ^ 1) for i in range(8)]
    chip_partial = partial + lax.ppermute(partial, "dp", swap)
    sent, chip_partial = lax.optimization_barrier((sent, chip_partial))
    received = lax.ppermute(sent, "dp", swap)
    gathered = [chip_partial] + [
        lax.ppermute(chip_partial, "dp", [(i, (i + 2 * k) % 8) for i in range(8)]) for k in range(1, 4)
    ]

    rows = CHIPS * BLOCK_ROWS
    chip_sum = pl.pallas_call(
        product_kernel,
        out_shape=jax.ShapeDtypeStruct((rows, LANES), F32),
        in_specs=[VMEM] * 8,
        out_specs=VMEM,
        compiler_params=PARAMS,
        cost_estimate=cost(10**7, 5 * 2**20),
    )(*gathered, received, *merged)
    both = ("dp", "tensor")
    chips = [[(2 * x + core) * 16 + t for x in range(3, -1, -1) for t in range(15, -1, -1)] for core in range(2)]
    blocks = lax.all_to_all(
        chip_sum.reshape(CHIPS, 1, BLOCK_ROWS * LANES), both, 0, 0, tiled=True, axis_index_groups=chips
    ).reshape(rows, LANES)

    copies, left = pl.pallas_call(
        solve_kernel,
        out_shape=[
            jax.ShapeDtypeStruct((CHIPS * 16, LANES), F32),
            jax.ShapeDtypeStruct((ROWS, LANES), F32),
        ],
        in_specs=[VMEM] * 5,
        out_specs=[VMEM] * 2,
        scratch_shapes=[pltpu.VMEM((16, LANES), F32)],
        compiler_params=PARAMS,
        cost_estimate=cost(10**6, 2**20),
    )(blocks, *gathered)
    mine = lax.all_to_all(
        copies.reshape(CHIPS, 1, 16 * LANES), both, 0, 0, tiled=True, axis_index_groups=chips
    ).reshape(CHIPS * 16, LANES)
    theirs = lax.ppermute(mine, "dp", swap)

    next_shapes = [jax.ShapeDtypeStruct((RANK, c), F32) for c in COLS]
    error_shapes = [jax.ShapeDtypeStruct((1, ROWS, c), BF16) for c in COLS]
    left_shapes = [jax.ShapeDtypeStruct((RANK, ROWS), F32)] * 3
    scratch = [pltpu.VMEM((RANK, c // 2), F32) for c in COLS] + [pltpu.VMEM((ROWS, c // 2), BF16) for c in COLS]
    sems = pltpu.SemaphoreType.DMA((sum(OUT_PIECES), 2))
    first = pl.pallas_call(
        functools.partial(finish_kernel, True),
        out_shape=next_shapes + error_shapes + left_shapes,
        in_specs=[VMEM] * 5,
        out_specs=[ANY] * 9,
        scratch_shapes=scratch
        + [sems, pltpu.VMEM((LANES, LANES), F32)]
        + [pltpu.VMEM((RANK, ROWS), F32)] * 3
        + [pltpu.SemaphoreType.DMA((3,))],
        compiler_params=PARAMS,
        cost_estimate=cost(10**7, 4 * 2**20),
    )(mine, left, *merged)
    lefts = first[6:9]
    second = pl.pallas_call(
        functools.partial(finish_kernel, False),
        out_shape=next_shapes + error_shapes,
        in_specs=[VMEM] * 5 + [ANY] * 6,
        out_specs=[ANY] * 6,
        scratch_shapes=scratch + [sems],
        input_output_aliases={5 + k: k for k in range(6)},
        compiler_params=PARAMS,
        cost_estimate=cost(10**7, 4 * 2**20),
    )(theirs, left, *merged, *first[0:6])
    return (*lefts, *second)


def solution(mesh):
    cut = P("dp", "tensor", None)
    return jax.shard_map(
        per_device,
        mesh=mesh,
        in_specs=(cut,) * 6 + (P(),) * 3,
        out_specs=(P(None, "tensor"),) * 3 + (P(),) * 3 + (cut,) * 3,
        check_vma=False,
    )
```

```python
import functools

import jax
import jax.numpy as jnp
from jax import lax
from jax.experimental import pallas as pl
from jax.experimental.pallas import tpu as pltpu
from jax.sharding import PartitionSpec as P

F32 = jnp.float32
BF16 = jnp.bfloat16
RANK = 4
ROWS = 16
LANES = 128
COLS = (28672, 28672, 8192)
BLOCK = 4 * LANES
OTHER_PIECES = ((0, 4096), (0, 10240), (1, 14336), (2, 4096))
OWN_PIECES = ((0, 14336), (2, 4096), (1, 10240), (1, 4096))
CHIPS = 64
BLOCK_ROWS = 17
HALF_BLOCKS = tuple(c // 2 // BLOCK for c in COLS)
FIRST_BLOCK = (0, HALF_BLOCKS[0], HALF_BLOCKS[0] + HALF_BLOCKS[1])
HALF = sum(COLS) // 2


def lane_iota(rows):
    return lax.broadcasted_iota(jnp.int32, (rows, LANES), 1)


def merge_kernel(*refs):
    grads, errors, rights = refs[0:3], refs[3:6], refs[6:9]
    merged, sent, partial = refs[9:12], refs[12], refs[13]
    gbuf, ebuf, rbuf, sems = refs[14:17], refs[17:20], refs[20:23], refs[23]
    core = lax.rem(lax.axis_index("dp"), 2)
    copies = []
    for own, pieces in ((False, OTHER_PIECES), (True, OWN_PIECES)):
        done = [0, 0, 0]
        for m, size in pieces:
            half = core if own else 1 - core
            start = pl.multiple_of(half * (COLS[m] // 2) + done[m], LANES)
            cols = pl.ds(start, size)
            index = len(copies)
            group = []
            if done[m] == 0:
                whole = pl.ds(start, COLS[m] // 2)
                group.append(pltpu.make_async_copy(rights[m].at[:, whole], rbuf[m].at[:, whole], sems.at[index, 2]))
            group.append(pltpu.make_async_copy(grads[m].at[0, :, cols], gbuf[m].at[:, cols], sems.at[index, 0]))
            group.append(pltpu.make_async_copy(errors[m].at[0, :, cols], ebuf[m].at[:, cols], sems.at[index, 1]))
            for copy in group:
                copy.start()
            copies.append((own, m, start, FIRST_BLOCK[m] * BLOCK + done[m], size, group))
            done[m] += size
    totals = [tuple(jnp.zeros((ROWS, LANES), F32) for _ in range(RANK)) for _ in range(3)]
    for own, m, start, place, size, group in copies:
        for copy in group:
            copy.wait()

        def step(j, acc, own=own, m=m, start=start, place=place):
            cols = pl.ds(pl.multiple_of(start + j * LANES, LANES), LANES)
            value = gbuf[m][:, cols] + ebuf[m][:, cols].astype(F32)
            merged[m][:, cols] = value
            if not own:
                sent[:, pl.ds(pl.multiple_of(place + j * LANES, LANES), LANES)] = value
            return tuple(acc[i] + value * rbuf[m][i : i + 1, cols] for i in range(RANK))

        totals[m] = lax.fori_loop(0, size // LANES, step, totals[m], unroll=16)
    lanes = lane_iota(ROWS)
    result = jnp.zeros((ROWS, LANES), F32)
    for m in range(3):
        for i in range(RANK):
            column = jnp.sum(totals[m][i], axis=1, keepdims=True)
            result = jnp.where(lanes == m * RANK + i, column, result)
    partial[...] = result


def sum_replicas(parts):
    return ((parts[0][...] + parts[2][...]) + (parts[1][...] + parts[3][...])) * 0.125


def fold(a, b, distance):
    mask = (lax.broadcasted_iota(jnp.int32, (8, LANES), 0) & distance) == 0
    return jnp.where(mask, a, b) + pltpu.roll(jnp.where(mask, b, a), 8 - distance, 0)


def product_kernel(*refs):
    gathered, received, merged, out = refs[0:4], refs[4], refs[5:8], refs[8]
    core = lax.rem(lax.axis_index("dp"), 2)
    left = sum_replicas(gathered)
    lanes = lane_iota(1)
    gram = jnp.zeros((1, LANES), F32)
    for shift in range(RANK):
        other = left if shift == 0 else pltpu.roll(left, LANES - shift, 1)
        row = jnp.where(lanes < 3 * RANK, jnp.sum(left * other, axis=0, keepdims=True), 0.0)
        gram = gram + (row if shift == 0 else pltpu.roll(row, 16 * shift, 1))
    for m in range(3):
        columns = [
            jnp.broadcast_to(left[:, m * RANK + i : m * RANK + i + 1], (ROWS, LANES)) for i in range(RANK)
        ]

        def step(block, carry, m=m, columns=columns):
            first = core * (COLS[m] // 2) + block * BLOCK
            place = (FIRST_BLOCK[m] + block) * BLOCK
            row = (FIRST_BLOCK[m] + block) * BLOCK_ROWS
            for pair in range(2):
                terms = []
                for b in range(2):
                    shift = (2 * pair + b) * LANES
                    mine = merged[m][:, pl.ds(pl.multiple_of(first + shift, LANES), LANES)]
                    value = mine + received[:, pl.ds(pl.multiple_of(place + shift, LANES), LANES)]
                    for i in range(RANK):
                        product = columns[i] * value
                        terms.append(product[:8] + product[8:])
                ones = [fold(terms[2 * k], terms[2 * k + 1], 1) for k in range(4)]
                twos = [fold(ones[2 * k], ones[2 * k + 1], 2) for k in range(2)]
                out[pl.ds(row + 8 * pair, 8), :] = fold(twos[0], twos[1], 4)
            out[pl.ds(row + 16, 1), :] = gram
            return carry

        lax.fori_loop(0, HALF_BLOCKS[m], step, 0, unroll=4)


def solve_kernel(blocks, *refs):
    gathered, copies, left_out, scratch = refs[0:4], refs[4], refs[5], refs[6]
    total = [jnp.zeros((16, LANES), F32) for _ in range(4)]
    grams = [jnp.zeros((1, LANES), F32) for _ in range(4)]
    for k in range(CHIPS):
        total[k % 4] = total[k % 4] + blocks[k * BLOCK_ROWS : k * BLOCK_ROWS + 16, :]
        grams[k % 4] = grams[k % 4] + blocks[k * BLOCK_ROWS + 16 : k * BLOCK_ROWS + 17, :]
    scratch[...] = (total[0] + total[1]) + (total[2] + total[3])
    gram = ((grams[0] + grams[1]) + (grams[2] + grams[3])) * 0.25

    def entry(i, j):
        shift = 16 * (i - j) + j
        return gram if shift == 0 else pltpu.roll(gram, LANES - shift, 1)

    factor = {}
    for j in range(RANK):
        for i in range(j, RANK):
            value = entry(i, j)
            for k in range(j):
                value = value - factor[i, k] * factor[j, k]
            factor[i, j] = jnp.sqrt(value) if i == j else value / factor[j, j]

    left_sum = sum_replicas(gathered)
    lanes = lane_iota(ROWS)
    valid = (lanes < 3 * RANK) & ((lanes & 3) == 0)
    rows, left = [], jnp.zeros((ROWS, LANES), F32)
    for i in range(RANK):
        current = left_sum if i == 0 else pltpu.roll(left_sum, LANES - i, 1)
        for j in range(i):
            current = current - factor[i, j] * rows[j]
        rows.append(current / factor[i, i])
        kept = jnp.where(valid, rows[i], 0.0)
        left = left + (kept if i == 0 else pltpu.roll(kept, i, 1))
    left_out[...] = left

    tensor = lax.axis_index("tensor")
    x, z, y = lax.div(lax.axis_index("dp"), 2), lax.div(tensor, 4), lax.rem(tensor, 4)
    mine = lax.rem(6 - x, 4) * 16 + lax.rem(6 - z, 4) * 4 + lax.rem(6 - y, 4)
    matrix = jnp.where(mine < FIRST_BLOCK[1], 0, jnp.where(mine < FIRST_BLOCK[2], 1, 2))
    one_lane = lane_iota(1) == matrix * RANK
    nexts = []
    for i in range(RANK):
        current = scratch[pl.ds(i, 4, stride=4), :] * 0.125
        for j in range(i):
            value = jnp.sum(jnp.where(one_lane, factor[i, j], 0.0), axis=1, keepdims=True)
            current = current - value * nexts[j]
        value = jnp.sum(jnp.where(one_lane, factor[i, i], 0.0), axis=1, keepdims=True)
        nexts.append(current / value)
    for i in range(RANK):
        scratch[pl.ds(i, 4, stride=4), :] = nexts[i]
    block = scratch[...]
    for k in range(CHIPS):
        copies[16 * k : 16 * k + 16, :] = block


OUT_PIECES = (4, 4, 1)


def finish_kernel(own, *refs):
    rows, left_ref, merged = refs[0], refs[1], refs[2:5]
    if own:
        nexts, errors, lefts = refs[5:8], refs[8:11], refs[11:14]
        nbuf, ebuf, sems, square, lbuf, lsems = refs[14:17], refs[17:20], refs[20], refs[21], refs[22:25], refs[25]
    else:
        nexts, errors = refs[11:14], refs[14:17]
        nbuf, ebuf, sems = refs[17:20], refs[20:23], refs[23]
    core = lax.rem(lax.axis_index("dp"), 2)
    half = core if own else 1 - core
    left = left_ref[...]
    copies = []
    if own:
        square[...] = jnp.zeros((LANES, LANES), F32)
        square[0:ROWS, :] = left
        turned = square[...].T
        for m in range(3):
            lbuf[m][...] = turned[m * RANK : (m + 1) * RANK, 0:ROWS]
            copy = pltpu.make_async_copy(lbuf[m], lefts[m], lsems.at[m])
            copy.start()
            copies.append(copy)
    index = 0
    for m in range(3):
        size = COLS[m] // 2 // OUT_PIECES[m]
        columns = [
            jnp.broadcast_to(left[:, m * RANK + i : m * RANK + i + 1], (ROWS, LANES)) for i in range(RANK)
        ]
        for piece in range(OUT_PIECES[m]):

            def step(j, carry, m=m, piece=piece, columns=columns, size=size):
                local = pl.multiple_of(piece * size + j * LANES, LANES)
                value = merged[m][:, pl.ds(pl.multiple_of(half * (COLS[m] // 2) + local, LANES), LANES)]
                row = FIRST_BLOCK[m] * 16 + piece * (size // LANES) * RANK + j * RANK
                nbuf[m][:, pl.ds(local, LANES)] = rows[pl.ds(row, RANK), :]
                approx = columns[0] * rows[pl.ds(row, 1), :]
                for i in range(1, RANK):
                    approx = approx + columns[i] * rows[pl.ds(row + i, 1), :]
                ebuf[m][:, pl.ds(local, LANES)] = (value - approx).astype(BF16)
                return carry

            lax.fori_loop(0, size // LANES, step, 0, unroll=14 if m < 2 else 16)
            here = pl.ds(piece * size, size)
            there = pl.ds(pl.multiple_of(half * (COLS[m] // 2) + piece * size, LANES), size)
            for copy in (
                pltpu.make_async_copy(ebuf[m].at[:, here], errors[m].at[0, :, there], sems.at[index, 0]),
                pltpu.make_async_copy(nbuf[m].at[:, here], nexts[m].at[:, there], sems.at[index, 1]),
            ):
                copy.start()
                copies.append(copy)
            index += 1
    for copy in copies:
        copy.wait()


ANY = pl.BlockSpec(memory_space=pl.ANY)
VMEM = pl.BlockSpec(memory_space=pltpu.VMEM)
PARAMS = pltpu.CompilerParams(vmem_limit_bytes=24 * 2**20)


def cost(flops, size):
    return pl.CostEstimate(flops=flops, bytes_accessed=size, transcendentals=0)


def per_device(*args):
    grads, errors, rights = args[0:3], args[3:6], args[6:9]
    grads, errors, rights = (
        [pltpu.with_memory_space_constraint(x, pltpu.HBM) for x in group] for group in (grads, errors, rights)
    )
    *merged, sent, partial = pl.pallas_call(
        merge_kernel,
        out_shape=[pltpu.VMEM((ROWS, c), F32) for c in COLS]
        + [jax.ShapeDtypeStruct((ROWS, HALF), F32), jax.ShapeDtypeStruct((ROWS, LANES), F32)],
        in_specs=[pl.BlockSpec(memory_space=pltpu.HBM)] * 9,
        out_specs=[VMEM] * 5,
        scratch_shapes=[pltpu.VMEM((ROWS, c), F32) for c in COLS]
        + [pltpu.VMEM((ROWS, c), BF16) for c in COLS]
        + [pltpu.VMEM((RANK, c), F32) for c in COLS]
        + [pltpu.SemaphoreType.DMA((len(OTHER_PIECES + OWN_PIECES), 3))],
        compiler_params=PARAMS,
        cost_estimate=cost(10**7, 7 * 2**20),
    )(*grads, *errors, *rights)
    swap = [(i, i ^ 1) for i in range(8)]
    chip_partial = partial + lax.ppermute(partial, "dp", swap)
    sent, chip_partial = lax.optimization_barrier((sent, chip_partial))
    received = lax.ppermute(sent, "dp", swap)
    gathered = [chip_partial] + [
        lax.ppermute(chip_partial, "dp", [(i, (i + 2 * k) % 8) for i in range(8)]) for k in range(1, 4)
    ]

    rows = CHIPS * BLOCK_ROWS
    chip_sum = pl.pallas_call(
        product_kernel,
        out_shape=jax.ShapeDtypeStruct((rows, LANES), F32),
        in_specs=[VMEM] * 8,
        out_specs=VMEM,
        compiler_params=PARAMS,
        cost_estimate=cost(10**7, 5 * 2**20),
    )(*gathered, received, *merged)
    both = ("dp", "tensor")
    down = (2, 1, 0, 3)
    chips = [[(2 * x + core) * 16 + z * 4 + y for x in down for z in down for y in down] for core in range(2)]
    blocks = lax.all_to_all(
        chip_sum.reshape(CHIPS, 1, BLOCK_ROWS * LANES), both, 0, 0, tiled=True, axis_index_groups=chips
    ).reshape(rows, LANES)

    copies, left = pl.pallas_call(
        solve_kernel,
        out_shape=[
            jax.ShapeDtypeStruct((CHIPS * 16, LANES), F32),
            jax.ShapeDtypeStruct((ROWS, LANES), F32),
        ],
        in_specs=[VMEM] * 5,
        out_specs=[VMEM] * 2,
        scratch_shapes=[pltpu.VMEM((16, LANES), F32)],
        compiler_params=PARAMS,
        cost_estimate=cost(10**6, 2**20),
    )(blocks, *gathered)
    mine = lax.all_to_all(
        copies.reshape(CHIPS, 1, 16 * LANES), both, 0, 0, tiled=True, axis_index_groups=chips
    ).reshape(CHIPS * 16, LANES)
    theirs = lax.ppermute(mine, "dp", swap)

    next_shapes = [jax.ShapeDtypeStruct((RANK, c), F32) for c in COLS]
    error_shapes = [jax.ShapeDtypeStruct((1, ROWS, c), BF16) for c in COLS]
    left_shapes = [jax.ShapeDtypeStruct((RANK, ROWS), F32)] * 3
    scratch = [pltpu.VMEM((RANK, c // 2), F32) for c in COLS] + [pltpu.VMEM((ROWS, c // 2), BF16) for c in COLS]
    sems = pltpu.SemaphoreType.DMA((sum(OUT_PIECES), 2))
    first = pl.pallas_call(
        functools.partial(finish_kernel, True),
        out_shape=next_shapes + error_shapes + left_shapes,
        in_specs=[VMEM] * 5,
        out_specs=[ANY] * 9,
        scratch_shapes=scratch
        + [sems, pltpu.VMEM((LANES, LANES), F32)]
        + [pltpu.VMEM((RANK, ROWS), F32)] * 3
        + [pltpu.SemaphoreType.DMA((3,))],
        compiler_params=PARAMS,
        cost_estimate=cost(10**7, 4 * 2**20),
    )(mine, left, *merged)
    lefts = first[6:9]
    second = pl.pallas_call(
        functools.partial(finish_kernel, False),
        out_shape=next_shapes + error_shapes,
        in_specs=[VMEM] * 5 + [ANY] * 6,
        out_specs=[ANY] * 6,
        scratch_shapes=scratch + [sems],
        input_output_aliases={5 + k: k for k in range(6)},
        compiler_params=PARAMS,
        cost_estimate=cost(10**7, 4 * 2**20),
    )(theirs, left, *merged, *first[0:6])
    return (*lefts, *second)


def solution(mesh):
    cut = P("dp", "tensor", None)
    return jax.shard_map(
        per_device,
        mesh=mesh,
        in_specs=(cut,) * 6 + (P(),) * 3,
        out_specs=(P(None, "tensor"),) * 3 + (P(),) * 3 + (cut,) * 3,
        check_vma=False,
    )
```

```python
import functools

import jax
import jax.numpy as jnp
from jax import lax
from jax.experimental import pallas as pl
from jax.experimental.pallas import tpu as pltpu
from jax.sharding import PartitionSpec as P

F32 = jnp.float32
BF16 = jnp.bfloat16
RANK = 4
ROWS = 16
LANES = 128
COLS = (28672, 28672, 8192)
BLOCK = 4 * LANES
OTHER_PIECES = ((0, 4096), (0, 10240), (1, 14336), (2, 4096))
OWN_PIECES = ((0, 14336), (2, 4096), (1, 10240), (1, 4096))
CHIPS = 64
BLOCK_ROWS = 17
HALF_BLOCKS = tuple(c // 2 // BLOCK for c in COLS)
FIRST_BLOCK = (0, HALF_BLOCKS[0], HALF_BLOCKS[0] + HALF_BLOCKS[1])
HALF = sum(COLS) // 2


def lane_iota(rows):
    return lax.broadcasted_iota(jnp.int32, (rows, LANES), 1)


def merge_kernel(*refs):
    grads, errors, rights = refs[0:3], refs[3:6], refs[6:9]
    merged, sent, partial = refs[9:12], refs[12], refs[13]
    gbuf, ebuf, rbuf, sems = refs[14:17], refs[17:20], refs[20:23], refs[23]
    core = lax.rem(lax.axis_index("dp"), 2)
    copies = []
    for own, pieces in ((False, OTHER_PIECES), (True, OWN_PIECES)):
        done = [0, 0, 0]
        for m, size in pieces:
            half = core if own else 1 - core
            start = pl.multiple_of(half * (COLS[m] // 2) + done[m], LANES)
            cols = pl.ds(start, size)
            index = len(copies)
            group = []
            if done[m] == 0:
                whole = pl.ds(start, COLS[m] // 2)
                group.append(pltpu.make_async_copy(rights[m].at[:, whole], rbuf[m].at[:, whole], sems.at[index, 2]))
            group.append(pltpu.make_async_copy(grads[m].at[0, :, cols], gbuf[m].at[:, cols], sems.at[index, 0]))
            group.append(pltpu.make_async_copy(errors[m].at[0, :, cols], ebuf[m].at[:, cols], sems.at[index, 1]))
            for copy in group:
                copy.start()
            copies.append((own, m, start, FIRST_BLOCK[m] * BLOCK + done[m], size, group))
            done[m] += size
    totals = [tuple(jnp.zeros((ROWS, LANES), F32) for _ in range(RANK)) for _ in range(3)]
    for own, m, start, place, size, group in copies:
        for copy in group:
            copy.wait()

        def step(j, acc, own=own, m=m, start=start, place=place):
            cols = pl.ds(pl.multiple_of(start + j * LANES, LANES), LANES)
            value = gbuf[m][:, cols] + ebuf[m][:, cols].astype(F32)
            merged[m][:, cols] = value
            if not own:
                sent[:, pl.ds(pl.multiple_of(place + j * LANES, LANES), LANES)] = value
            return tuple(acc[i] + value * rbuf[m][i : i + 1, cols] for i in range(RANK))

        totals[m] = lax.fori_loop(0, size // LANES, step, totals[m], unroll=16)
    lanes = lane_iota(ROWS)
    result = jnp.zeros((ROWS, LANES), F32)
    for m in range(3):
        for i in range(RANK):
            column = jnp.sum(totals[m][i], axis=1, keepdims=True)
            result = jnp.where(lanes == m * RANK + i, column, result)
    partial[...] = result


def sum_replicas(parts):
    return ((parts[0][...] + parts[2][...]) + (parts[1][...] + parts[3][...])) * 0.125


def split_kernel(received, *refs):
    merged, parts = refs[0:3], refs[3]
    core = lax.rem(lax.axis_index("dp"), 2)
    for m in range(3):

        def step(j, carry, m=m):
            here = pl.ds(pl.multiple_of(FIRST_BLOCK[m] * BLOCK + j * LANES, LANES), LANES)
            mine = merged[m][:, pl.ds(pl.multiple_of(core * (COLS[m] // 2) + j * LANES, LANES), LANES)]
            value = mine + received[:, here]
            high = value.astype(BF16)
            parts[0:ROWS, here] = high
            parts[ROWS : 2 * ROWS, here] = (value - high.astype(F32)).astype(BF16)
            return carry

        lax.fori_loop(0, COLS[m] // 2 // LANES, step, 0, unroll=16)


def product_kernel(*refs):
    gathered, parts, out, square = refs[0:4], refs[4], refs[5], refs[6]
    left = sum_replicas(gathered)
    square[...] = jnp.zeros((LANES, LANES), F32)
    square[0:ROWS, :] = left
    turned = square[...].T[0 : 3 * RANK, 0:ROWS]
    high = turned.astype(BF16).astype(F32)
    low = turned - high
    for m in range(3):
        mine = slice(m * RANK, (m + 1) * RANK)
        factors = jnp.concatenate(
            [
                jnp.concatenate([high[mine], high[mine]], axis=1),
                jnp.concatenate([low[mine], low[mine]], axis=1),
            ],
            axis=0,
        ).astype(BF16)
        start = FIRST_BLOCK[m] * BLOCK
        both = jnp.dot(factors, parts[:, start : start + COLS[m] // 2], preferred_element_type=F32)
        for j in range(COLS[m] // 2 // LANES):
            place = FIRST_BLOCK[m] * 4 + j
            row = place // 4 * BLOCK_ROWS + place % 4 * RANK
            value = both[:, j * LANES : (j + 1) * LANES]
            out[row : row + RANK, :] = value[0:RANK] + value[RANK : 2 * RANK]
    lanes = lane_iota(1)
    gram = jnp.zeros((1, LANES), F32)
    for shift in range(RANK):
        other = left if shift == 0 else pltpu.roll(left, LANES - shift, 1)
        row = jnp.where(lanes < 3 * RANK, jnp.sum(left * other, axis=0, keepdims=True), 0.0)
        gram = gram + (row if shift == 0 else pltpu.roll(row, 16 * shift, 1))
    for k in range(CHIPS):
        out[k * BLOCK_ROWS + 16 : (k + 1) * BLOCK_ROWS, :] = gram


def solve_kernel(blocks, *refs):
    gathered, copies, left_out, scratch = refs[0:4], refs[4], refs[5], refs[6]
    total = [jnp.zeros((16, LANES), F32) for _ in range(4)]
    grams = [jnp.zeros((1, LANES), F32) for _ in range(4)]
    for k in range(CHIPS):
        total[k % 4] = total[k % 4] + blocks[k * BLOCK_ROWS : k * BLOCK_ROWS + 16, :]
        grams[k % 4] = grams[k % 4] + blocks[k * BLOCK_ROWS + 16 : k * BLOCK_ROWS + 17, :]
    scratch[...] = (total[0] + total[1]) + (total[2] + total[3])
    gram = ((grams[0] + grams[1]) + (grams[2] + grams[3])) * 0.25

    def entry(i, j):
        shift = 16 * (i - j) + j
        return gram if shift == 0 else pltpu.roll(gram, LANES - shift, 1)

    factor = {}
    for j in range(RANK):
        for i in range(j, RANK):
            value = entry(i, j)
            for k in range(j):
                value = value - factor[i, k] * factor[j, k]
            factor[i, j] = jnp.sqrt(value) if i == j else value / factor[j, j]

    left_sum = sum_replicas(gathered)
    lanes = lane_iota(ROWS)
    valid = (lanes < 3 * RANK) & ((lanes & 3) == 0)
    rows, left = [], jnp.zeros((ROWS, LANES), F32)
    for i in range(RANK):
        current = left_sum if i == 0 else pltpu.roll(left_sum, LANES - i, 1)
        for j in range(i):
            current = current - factor[i, j] * rows[j]
        rows.append(current / factor[i, i])
        kept = jnp.where(valid, rows[i], 0.0)
        left = left + (kept if i == 0 else pltpu.roll(kept, i, 1))
    left_out[...] = left

    tensor = lax.axis_index("tensor")
    x, z, y = lax.div(lax.axis_index("dp"), 2), lax.div(tensor, 4), lax.rem(tensor, 4)
    mine = lax.rem(6 - x, 4) * 16 + lax.rem(6 - z, 4) * 4 + lax.rem(6 - y, 4)
    matrix = jnp.where(mine < FIRST_BLOCK[1], 0, jnp.where(mine < FIRST_BLOCK[2], 1, 2))
    one_lane = lane_iota(1) == matrix * RANK
    nexts = []
    for i in range(RANK):
        current = scratch[pl.ds(i, 4, stride=4), :] * 0.125
        for j in range(i):
            value = jnp.sum(jnp.where(one_lane, factor[i, j], 0.0), axis=1, keepdims=True)
            current = current - value * nexts[j]
        value = jnp.sum(jnp.where(one_lane, factor[i, i], 0.0), axis=1, keepdims=True)
        nexts.append(current / value)
    for i in range(RANK):
        scratch[pl.ds(i, 4, stride=4), :] = nexts[i]
    block = scratch[...]
    for k in range(CHIPS):
        copies[16 * k : 16 * k + 16, :] = block


OUT_PIECES = (4, 4, 1)


def finish_kernel(own, *refs):
    rows, left_ref, merged = refs[0], refs[1], refs[2:5]
    if own:
        nexts, errors, lefts = refs[5:8], refs[8:11], refs[11:14]
        nbuf, ebuf, sems, square, lbuf, lsems = refs[14:17], refs[17:20], refs[20], refs[21], refs[22:25], refs[25]
    else:
        nexts, errors = refs[11:14], refs[14:17]
        nbuf, ebuf, sems = refs[17:20], refs[20:23], refs[23]
    core = lax.rem(lax.axis_index("dp"), 2)
    half = core if own else 1 - core
    left = left_ref[...]
    copies = []
    if own:
        square[...] = jnp.zeros((LANES, LANES), F32)
        square[0:ROWS, :] = left
        turned = square[...].T
        for m in range(3):
            lbuf[m][...] = turned[m * RANK : (m + 1) * RANK, 0:ROWS]
            copy = pltpu.make_async_copy(lbuf[m], lefts[m], lsems.at[m])
            copy.start()
            copies.append(copy)
    index = 0
    for m in range(3):
        size = COLS[m] // 2 // OUT_PIECES[m]
        columns = [
            jnp.broadcast_to(left[:, m * RANK + i : m * RANK + i + 1], (ROWS, LANES)) for i in range(RANK)
        ]
        for piece in range(OUT_PIECES[m]):

            def step(j, carry, m=m, piece=piece, columns=columns, size=size):
                local = pl.multiple_of(piece * size + j * LANES, LANES)
                value = merged[m][:, pl.ds(pl.multiple_of(half * (COLS[m] // 2) + local, LANES), LANES)]
                row = FIRST_BLOCK[m] * 16 + piece * (size // LANES) * RANK + j * RANK
                nbuf[m][:, pl.ds(local, LANES)] = rows[pl.ds(row, RANK), :]
                approx = columns[0] * rows[pl.ds(row, 1), :]
                for i in range(1, RANK):
                    approx = approx + columns[i] * rows[pl.ds(row + i, 1), :]
                ebuf[m][:, pl.ds(local, LANES)] = (value - approx).astype(BF16)
                return carry

            lax.fori_loop(0, size // LANES, step, 0, unroll=14 if m < 2 else 16)
            here = pl.ds(piece * size, size)
            there = pl.ds(pl.multiple_of(half * (COLS[m] // 2) + piece * size, LANES), size)
            for copy in (
                pltpu.make_async_copy(ebuf[m].at[:, here], errors[m].at[0, :, there], sems.at[index, 0]),
                pltpu.make_async_copy(nbuf[m].at[:, here], nexts[m].at[:, there], sems.at[index, 1]),
            ):
                copy.start()
                copies.append(copy)
            index += 1
    for copy in copies:
        copy.wait()


ANY = pl.BlockSpec(memory_space=pl.ANY)
VMEM = pl.BlockSpec(memory_space=pltpu.VMEM)
PARAMS = pltpu.CompilerParams(vmem_limit_bytes=24 * 2**20)


def cost(flops, size):
    return pl.CostEstimate(flops=flops, bytes_accessed=size, transcendentals=0)


def per_device(*args):
    grads, errors, rights = args[0:3], args[3:6], args[6:9]
    grads, errors, rights = (
        [pltpu.with_memory_space_constraint(x, pltpu.HBM) for x in group] for group in (grads, errors, rights)
    )
    *merged, sent, partial = pl.pallas_call(
        merge_kernel,
        out_shape=[pltpu.VMEM((ROWS, c), F32) for c in COLS]
        + [jax.ShapeDtypeStruct((ROWS, HALF), F32), jax.ShapeDtypeStruct((ROWS, LANES), F32)],
        in_specs=[pl.BlockSpec(memory_space=pltpu.HBM)] * 9,
        out_specs=[VMEM] * 5,
        scratch_shapes=[pltpu.VMEM((ROWS, c), F32) for c in COLS]
        + [pltpu.VMEM((ROWS, c), BF16) for c in COLS]
        + [pltpu.VMEM((RANK, c), F32) for c in COLS]
        + [pltpu.SemaphoreType.DMA((len(OTHER_PIECES + OWN_PIECES), 3))],
        compiler_params=PARAMS,
        cost_estimate=cost(10**7, 7 * 2**20),
    )(*grads, *errors, *rights)
    swap = [(i, i ^ 1) for i in range(8)]
    chip_partial = partial + lax.ppermute(partial, "dp", swap)
    sent, chip_partial = lax.optimization_barrier((sent, chip_partial))
    received = lax.ppermute(sent, "dp", swap)
    gathered = [chip_partial] + [
        lax.ppermute(chip_partial, "dp", [(i, (i + 2 * k) % 8) for i in range(8)]) for k in range(1, 4)
    ]

    rows = CHIPS * BLOCK_ROWS
    parts = pl.pallas_call(
        split_kernel,
        out_shape=jax.ShapeDtypeStruct((2 * ROWS, HALF), BF16),
        in_specs=[VMEM] * 4,
        out_specs=VMEM,
        compiler_params=PARAMS,
        cost_estimate=cost(10**7, 6 * 2**20),
    )(received, *merged)
    chip_sum = pl.pallas_call(
        product_kernel,
        out_shape=jax.ShapeDtypeStruct((rows, LANES), F32),
        in_specs=[VMEM] * 5,
        out_specs=VMEM,
        scratch_shapes=[pltpu.VMEM((LANES, LANES), F32)],
        compiler_params=PARAMS,
        cost_estimate=cost(10**7, 3 * 2**20),
    )(*gathered, parts)
    both = ("dp", "tensor")
    down = (2, 1, 0, 3)
    chips = [[(2 * x + core) * 16 + z * 4 + y for x in down for z in down for y in down] for core in range(2)]
    blocks = lax.all_to_all(
        chip_sum.reshape(CHIPS, 1, BLOCK_ROWS * LANES), both, 0, 0, tiled=True, axis_index_groups=chips
    ).reshape(rows, LANES)

    copies, left = pl.pallas_call(
        solve_kernel,
        out_shape=[
            jax.ShapeDtypeStruct((CHIPS * 16, LANES), F32),
            jax.ShapeDtypeStruct((ROWS, LANES), F32),
        ],
        in_specs=[VMEM] * 5,
        out_specs=[VMEM] * 2,
        scratch_shapes=[pltpu.VMEM((16, LANES), F32)],
        compiler_params=PARAMS,
        cost_estimate=cost(10**6, 2**20),
    )(blocks, *gathered)
    mine = lax.all_to_all(
        copies.reshape(CHIPS, 1, 16 * LANES), both, 0, 0, tiled=True, axis_index_groups=chips
    ).reshape(CHIPS * 16, LANES)
    theirs = lax.ppermute(mine, "dp", swap)

    next_shapes = [jax.ShapeDtypeStruct((RANK, c), F32) for c in COLS]
    error_shapes = [jax.ShapeDtypeStruct((1, ROWS, c), BF16) for c in COLS]
    left_shapes = [jax.ShapeDtypeStruct((RANK, ROWS), F32)] * 3
    scratch = [pltpu.VMEM((RANK, c // 2), F32) for c in COLS] + [pltpu.VMEM((ROWS, c // 2), BF16) for c in COLS]
    sems = pltpu.SemaphoreType.DMA((sum(OUT_PIECES), 2))
    first = pl.pallas_call(
        functools.partial(finish_kernel, True),
        out_shape=next_shapes + error_shapes + left_shapes,
        in_specs=[VMEM] * 5,
        out_specs=[ANY] * 9,
        scratch_shapes=scratch
        + [sems, pltpu.VMEM((LANES, LANES), F32)]
        + [pltpu.VMEM((RANK, ROWS), F32)] * 3
        + [pltpu.SemaphoreType.DMA((3,))],
        compiler_params=PARAMS,
        cost_estimate=cost(10**7, 4 * 2**20),
    )(mine, left, *merged)
    lefts = first[6:9]
    second = pl.pallas_call(
        functools.partial(finish_kernel, False),
        out_shape=next_shapes + error_shapes,
        in_specs=[VMEM] * 5 + [ANY] * 6,
        out_specs=[ANY] * 6,
        scratch_shapes=scratch + [sems],
        input_output_aliases={5 + k: k for k in range(6)},
        compiler_params=PARAMS,
        cost_estimate=cost(10**7, 4 * 2**20),
    )(theirs, left, *merged, *first[0:6])
    return (*lefts, *second)


def solution(mesh):
    cut = P("dp", "tensor", None)
    return jax.shard_map(
        per_device,
        mesh=mesh,
        in_specs=(cut,) * 6 + (P(),) * 3,
        out_specs=(P(None, "tensor"),) * 3 + (P(),) * 3 + (cut,) * 3,
        check_vma=False,
    )
```

```python
import functools

import jax
import jax.numpy as jnp
from jax import lax
from jax.experimental import pallas as pl
from jax.experimental.pallas import tpu as pltpu
from jax.sharding import PartitionSpec as P

F32 = jnp.float32
BF16 = jnp.bfloat16
RANK = 4
ROWS = 16
LANES = 128
COLS = (28672, 28672, 8192)
BLOCK = 4 * LANES
OTHER_PIECES = ((0, 4096), (0, 10240), (1, 14336), (2, 4096))
OWN_PIECES = ((0, 14336), (2, 4096), (1, 10240), (1, 4096))
CHIPS = 64
BLOCK_ROWS = 17
HALF_BLOCKS = tuple(c // 2 // BLOCK for c in COLS)
FIRST_BLOCK = (0, HALF_BLOCKS[0], HALF_BLOCKS[0] + HALF_BLOCKS[1])
HALF = sum(COLS) // 2


def lane_iota(rows):
    return lax.broadcasted_iota(jnp.int32, (rows, LANES), 1)


def merge_kernel(*refs):
    grads, errors, rights = refs[0:3], refs[3:6], refs[6:9]
    merged, sent, partial = refs[9:12], refs[12], refs[13]
    gbuf, ebuf, rbuf, sems = refs[14:17], refs[17:20], refs[20:23], refs[23]
    core = lax.rem(lax.axis_index("dp"), 2)
    copies = []
    for own, pieces in ((False, OTHER_PIECES), (True, OWN_PIECES)):
        done = [0, 0, 0]
        for m, size in pieces:
            half = core if own else 1 - core
            start = pl.multiple_of(half * (COLS[m] // 2) + done[m], LANES)
            cols = pl.ds(start, size)
            index = len(copies)
            group = []
            if done[m] == 0:
                whole = pl.ds(start, COLS[m] // 2)
                group.append(pltpu.make_async_copy(rights[m].at[:, whole], rbuf[m].at[:, whole], sems.at[index, 2]))
            group.append(pltpu.make_async_copy(grads[m].at[0, :, cols], gbuf[m].at[:, cols], sems.at[index, 0]))
            group.append(pltpu.make_async_copy(errors[m].at[0, :, cols], ebuf[m].at[:, cols], sems.at[index, 1]))
            for copy in group:
                copy.start()
            copies.append((own, m, start, FIRST_BLOCK[m] * BLOCK + done[m], size, group))
            done[m] += size
    totals = [tuple(jnp.zeros((ROWS, LANES), F32) for _ in range(RANK)) for _ in range(3)]
    for own, m, start, place, size, group in copies:
        for copy in group:
            copy.wait()

        def step(j, acc, own=own, m=m, start=start, place=place):
            cols = pl.ds(pl.multiple_of(start + j * LANES, LANES), LANES)
            value = gbuf[m][:, cols] + ebuf[m][:, cols].astype(F32)
            merged[m][:, cols] = value
            if not own:
                sent[:, pl.ds(pl.multiple_of(place + j * LANES, LANES), LANES)] = value
            return tuple(acc[i] + value * rbuf[m][i : i + 1, cols] for i in range(RANK))

        totals[m] = lax.fori_loop(0, size // LANES, step, totals[m], unroll=16)
    lanes = lane_iota(ROWS)
    result = jnp.zeros((ROWS, LANES), F32)
    for m in range(3):
        for i in range(RANK):
            column = jnp.sum(totals[m][i], axis=1, keepdims=True)
            result = jnp.where(lanes == m * RANK + i, column, result)
    partial[...] = result


def sum_replicas(parts):
    return ((parts[0][...] + parts[2][...]) + (parts[1][...] + parts[3][...])) * 0.125


def split_kernel(received, *refs):
    merged, parts = refs[0:3], refs[3]
    core = lax.rem(lax.axis_index("dp"), 2)
    for m in range(3):

        def step(j, carry, m=m):
            here = pl.ds(pl.multiple_of(FIRST_BLOCK[m] * BLOCK + j * LANES, LANES), LANES)
            mine = merged[m][:, pl.ds(pl.multiple_of(core * (COLS[m] // 2) + j * LANES, LANES), LANES)]
            value = mine + received[:, here]
            high = value.astype(BF16)
            parts[0:ROWS, here] = high
            parts[ROWS : 2 * ROWS, here] = (value - high.astype(F32)).astype(BF16)
            return carry

        lax.fori_loop(0, COLS[m] // 2 // LANES, step, 0, unroll=16)


def product_kernel(*refs):
    gathered, parts, out, square = refs[0:4], refs[4], refs[5], refs[6]
    left = sum_replicas(gathered)
    square[...] = jnp.zeros((LANES, LANES), F32)
    square[0:ROWS, :] = left
    turned = square[...].T[0 : 3 * RANK, 0:ROWS]
    high = turned.astype(BF16).astype(F32)
    low = turned - high
    for m in range(3):
        mine = slice(m * RANK, (m + 1) * RANK)
        factors = jnp.concatenate(
            [
                jnp.concatenate([high[mine], high[mine]], axis=1),
                jnp.concatenate([low[mine], low[mine]], axis=1),
            ],
            axis=0,
        ).astype(BF16)
        start = FIRST_BLOCK[m] * BLOCK
        both = jnp.dot(factors, parts[:, start : start + COLS[m] // 2], preferred_element_type=F32)
        for j in range(COLS[m] // 2 // LANES):
            place = FIRST_BLOCK[m] * 4 + j
            row = place // 4 * BLOCK_ROWS + place % 4 * RANK
            value = both[:, j * LANES : (j + 1) * LANES]
            out[row : row + RANK, :] = value[0:RANK] + value[RANK : 2 * RANK]
    lanes = lane_iota(1)
    gram = jnp.zeros((1, LANES), F32)
    for shift in range(RANK):
        other = left if shift == 0 else pltpu.roll(left, LANES - shift, 1)
        row = jnp.where(lanes < 3 * RANK, jnp.sum(left * other, axis=0, keepdims=True), 0.0)
        gram = gram + (row if shift == 0 else pltpu.roll(row, 16 * shift, 1))
    for k in range(CHIPS):
        out[k * BLOCK_ROWS + 16 : (k + 1) * BLOCK_ROWS, :] = gram


def solve_kernel(blocks, *refs):
    gathered, copies, left_out, scratch = refs[0:4], refs[4], refs[5], refs[6]
    total = [jnp.zeros((16, LANES), F32) for _ in range(4)]
    grams = [jnp.zeros((1, LANES), F32) for _ in range(4)]
    for k in range(CHIPS):
        total[k % 4] = total[k % 4] + blocks[k * BLOCK_ROWS : k * BLOCK_ROWS + 16, :]
        grams[k % 4] = grams[k % 4] + blocks[k * BLOCK_ROWS + 16 : k * BLOCK_ROWS + 17, :]
    scratch[...] = (total[0] + total[1]) + (total[2] + total[3])
    gram = ((grams[0] + grams[1]) + (grams[2] + grams[3])) * 0.25

    def entry(i, j):
        shift = 16 * (i - j) + j
        return gram if shift == 0 else pltpu.roll(gram, LANES - shift, 1)

    factor = {}
    for j in range(RANK):
        for i in range(j, RANK):
            value = entry(i, j)
            for k in range(j):
                value = value - factor[i, k] * factor[j, k]
            factor[i, j] = jnp.sqrt(value) if i == j else value / factor[j, j]

    left_sum = sum_replicas(gathered)
    lanes = lane_iota(ROWS)
    valid = (lanes < 3 * RANK) & ((lanes & 3) == 0)
    rows, left = [], jnp.zeros((ROWS, LANES), F32)
    for i in range(RANK):
        current = left_sum if i == 0 else pltpu.roll(left_sum, LANES - i, 1)
        for j in range(i):
            current = current - factor[i, j] * rows[j]
        rows.append(current / factor[i, i])
        kept = jnp.where(valid, rows[i], 0.0)
        left = left + (kept if i == 0 else pltpu.roll(kept, i, 1))
    left_out[...] = left

    tensor = lax.axis_index("tensor")
    x, z, y = lax.div(lax.axis_index("dp"), 2), lax.div(tensor, 4), lax.rem(tensor, 4)
    mine = lax.rem(6 - x, 4) * 16 + lax.rem(6 - z, 4) * 4 + lax.rem(6 - y, 4)
    matrix = jnp.where(mine < FIRST_BLOCK[1], 0, jnp.where(mine < FIRST_BLOCK[2], 1, 2))
    one_lane = lane_iota(1) == matrix * RANK
    nexts = []
    for i in range(RANK):
        current = scratch[pl.ds(i, 4, stride=4), :] * 0.125
        for j in range(i):
            value = jnp.sum(jnp.where(one_lane, factor[i, j], 0.0), axis=1, keepdims=True)
            current = current - value * nexts[j]
        value = jnp.sum(jnp.where(one_lane, factor[i, i], 0.0), axis=1, keepdims=True)
        nexts.append(current / value)
    for i in range(RANK):
        scratch[pl.ds(i, 4, stride=4), :] = nexts[i]
    block = scratch[...]
    for k in range(CHIPS):
        copies[16 * k : 16 * k + 16, :] = block


OUT_PIECES = (1, 1, 1)


def finish_kernel(own, *refs):
    rows, left_ref, merged = refs[0], refs[1], refs[2:5]
    if own:
        nexts, errors, lefts = refs[5:8], refs[8:11], refs[11:14]
        nbuf, ebuf, sems, square, lbuf, lsems = refs[14:17], refs[17:20], refs[20], refs[21], refs[22:25], refs[25]
    else:
        nexts, errors = refs[11:14], refs[14:17]
        nbuf, ebuf, sems = refs[17:20], refs[20:23], refs[23]
    core = lax.rem(lax.axis_index("dp"), 2)
    half = core if own else 1 - core
    left = left_ref[...]
    copies = []
    if own:
        square[...] = jnp.zeros((LANES, LANES), F32)
        square[0:ROWS, :] = left
        turned = square[...].T
        for m in range(3):
            lbuf[m][...] = turned[m * RANK : (m + 1) * RANK, 0:ROWS]
            copy = pltpu.make_async_copy(lbuf[m], lefts[m], lsems.at[m])
            copy.start()
            copies.append(copy)
    index = 0
    for m in range(3):
        size = COLS[m] // 2 // OUT_PIECES[m]
        columns = [
            jnp.broadcast_to(left[:, m * RANK + i : m * RANK + i + 1], (ROWS, LANES)) for i in range(RANK)
        ]
        for piece in range(OUT_PIECES[m]):

            def step(j, carry, m=m, piece=piece, columns=columns, size=size):
                local = pl.multiple_of(piece * size + j * LANES, LANES)
                value = merged[m][:, pl.ds(pl.multiple_of(half * (COLS[m] // 2) + local, LANES), LANES)]
                row = FIRST_BLOCK[m] * 16 + piece * (size // LANES) * RANK + j * RANK
                nbuf[m][:, pl.ds(local, LANES)] = rows[pl.ds(row, RANK), :]
                approx = columns[0] * rows[pl.ds(row, 1), :]
                for i in range(1, RANK):
                    approx = approx + columns[i] * rows[pl.ds(row + i, 1), :]
                ebuf[m][:, pl.ds(local, LANES)] = (value - approx).astype(BF16)
                return carry

            lax.fori_loop(0, size // LANES, step, 0, unroll=14 if m < 2 else 16)
            here = pl.ds(piece * size, size)
            there = pl.ds(pl.multiple_of(half * (COLS[m] // 2) + piece * size, LANES), size)
            for copy in (
                pltpu.make_async_copy(ebuf[m].at[:, here], errors[m].at[0, :, there], sems.at[index, 0]),
                pltpu.make_async_copy(nbuf[m].at[:, here], nexts[m].at[:, there], sems.at[index, 1]),
            ):
                copy.start()
                copies.append(copy)
            index += 1
    for copy in copies:
        copy.wait()


ANY = pl.BlockSpec(memory_space=pl.ANY)
VMEM = pl.BlockSpec(memory_space=pltpu.VMEM)
PARAMS = pltpu.CompilerParams(vmem_limit_bytes=24 * 2**20)


def cost(flops, size):
    return pl.CostEstimate(flops=flops, bytes_accessed=size, transcendentals=0)


def per_device(*args):
    grads, errors, rights = args[0:3], args[3:6], args[6:9]
    grads, errors, rights = (
        [pltpu.with_memory_space_constraint(x, pltpu.HBM) for x in group] for group in (grads, errors, rights)
    )
    *merged, sent, partial = pl.pallas_call(
        merge_kernel,
        out_shape=[pltpu.VMEM((ROWS, c), F32) for c in COLS]
        + [jax.ShapeDtypeStruct((ROWS, HALF), F32), jax.ShapeDtypeStruct((ROWS, LANES), F32)],
        in_specs=[pl.BlockSpec(memory_space=pltpu.HBM)] * 9,
        out_specs=[VMEM] * 5,
        scratch_shapes=[pltpu.VMEM((ROWS, c), F32) for c in COLS]
        + [pltpu.VMEM((ROWS, c), BF16) for c in COLS]
        + [pltpu.VMEM((RANK, c), F32) for c in COLS]
        + [pltpu.SemaphoreType.DMA((len(OTHER_PIECES + OWN_PIECES), 3))],
        compiler_params=PARAMS,
        cost_estimate=cost(10**7, 7 * 2**20),
    )(*grads, *errors, *rights)
    swap = [(i, i ^ 1) for i in range(8)]
    chip_partial = partial + lax.ppermute(partial, "dp", swap)
    sent, chip_partial = lax.optimization_barrier((sent, chip_partial))
    received = lax.ppermute(sent, "dp", swap)
    gathered = [chip_partial] + [
        lax.ppermute(chip_partial, "dp", [(i, (i + 2 * k) % 8) for i in range(8)]) for k in range(1, 4)
    ]

    rows = CHIPS * BLOCK_ROWS
    parts = pl.pallas_call(
        split_kernel,
        out_shape=jax.ShapeDtypeStruct((2 * ROWS, HALF), BF16),
        in_specs=[VMEM] * 4,
        out_specs=VMEM,
        compiler_params=PARAMS,
        cost_estimate=cost(10**7, 6 * 2**20),
    )(received, *merged)
    chip_sum = pl.pallas_call(
        product_kernel,
        out_shape=jax.ShapeDtypeStruct((rows, LANES), F32),
        in_specs=[VMEM] * 5,
        out_specs=VMEM,
        scratch_shapes=[pltpu.VMEM((LANES, LANES), F32)],
        compiler_params=PARAMS,
        cost_estimate=cost(10**7, 3 * 2**20),
    )(*gathered, parts)
    both = ("dp", "tensor")
    down = (2, 1, 0, 3)
    chips = [[(2 * x + core) * 16 + z * 4 + y for x in down for z in down for y in down] for core in range(2)]
    blocks = lax.all_to_all(
        chip_sum.reshape(CHIPS, 1, BLOCK_ROWS * LANES), both, 0, 0, tiled=True, axis_index_groups=chips
    ).reshape(rows, LANES)

    copies, left = pl.pallas_call(
        solve_kernel,
        out_shape=[
            jax.ShapeDtypeStruct((CHIPS * 16, LANES), F32),
            jax.ShapeDtypeStruct((ROWS, LANES), F32),
        ],
        in_specs=[VMEM] * 5,
        out_specs=[VMEM] * 2,
        scratch_shapes=[pltpu.VMEM((16, LANES), F32)],
        compiler_params=PARAMS,
        cost_estimate=cost(10**6, 2**20),
    )(blocks, *gathered)
    mine = lax.all_to_all(
        copies.reshape(CHIPS, 1, 16 * LANES), both, 0, 0, tiled=True, axis_index_groups=chips
    ).reshape(CHIPS * 16, LANES)
    theirs = lax.ppermute(mine, "dp", swap)

    next_shapes = [jax.ShapeDtypeStruct((RANK, c), F32) for c in COLS]
    error_shapes = [jax.ShapeDtypeStruct((1, ROWS, c), BF16) for c in COLS]
    left_shapes = [jax.ShapeDtypeStruct((RANK, ROWS), F32)] * 3
    scratch = [pltpu.VMEM((RANK, c // 2), F32) for c in COLS] + [pltpu.VMEM((ROWS, c // 2), BF16) for c in COLS]
    sems = pltpu.SemaphoreType.DMA((sum(OUT_PIECES), 2))
    first = pl.pallas_call(
        functools.partial(finish_kernel, True),
        out_shape=next_shapes + error_shapes + left_shapes,
        in_specs=[VMEM] * 5,
        out_specs=[ANY] * 9,
        scratch_shapes=scratch
        + [sems, pltpu.VMEM((LANES, LANES), F32)]
        + [pltpu.VMEM((RANK, ROWS), F32)] * 3
        + [pltpu.SemaphoreType.DMA((3,))],
        compiler_params=PARAMS,
        cost_estimate=cost(10**7, 4 * 2**20),
    )(mine, left, *merged)
    lefts = first[6:9]
    second = pl.pallas_call(
        functools.partial(finish_kernel, False),
        out_shape=next_shapes + error_shapes,
        in_specs=[VMEM] * 5 + [ANY] * 6,
        out_specs=[ANY] * 6,
        scratch_shapes=scratch + [sems],
        input_output_aliases={5 + k: k for k in range(6)},
        compiler_params=PARAMS,
        cost_estimate=cost(10**7, 4 * 2**20),
    )(theirs, left, *merged, *first[0:6])
    return (*lefts, *second)


def solution(mesh):
    cut = P("dp", "tensor", None)
    return jax.shard_map(
        per_device,
        mesh=mesh,
        in_specs=(cut,) * 6 + (P(),) * 3,
        out_specs=(P(None, "tensor"),) * 3 + (P(),) * 3 + (cut,) * 3,
        check_vma=False,
    )
```

```python
import functools

import jax
import jax.numpy as jnp
from jax import lax
from jax.experimental import pallas as pl
from jax.experimental.pallas import tpu as pltpu
from jax.sharding import PartitionSpec as P

F32 = jnp.float32
BF16 = jnp.bfloat16
RANK = 4
ROWS = 16
LANES = 128
COLS = (28672, 28672, 8192)
BLOCK = 4 * LANES
OTHER_PIECES = ((0, 4096), (0, 10240), (1, 14336), (2, 4096))
OWN_PIECES = ((0, 14336), (2, 4096), (1, 10240), (1, 4096))
CHIPS = 64
BLOCK_ROWS = 17
HALF_BLOCKS = tuple(c // 2 // BLOCK for c in COLS)
FIRST_BLOCK = (0, HALF_BLOCKS[0], HALF_BLOCKS[0] + HALF_BLOCKS[1])
HALF = sum(COLS) // 2


def lane_iota(rows):
    return lax.broadcasted_iota(jnp.int32, (rows, LANES), 1)


def merge_kernel(*refs):
    grads, errors, rights = refs[0:3], refs[3:6], refs[6:9]
    merged, sent, partial = refs[9:12], refs[12], refs[13]
    gbuf, ebuf, rbuf, sems = refs[14:17], refs[17:20], refs[20:23], refs[23]
    core = lax.rem(lax.axis_index("dp"), 2)
    copies = []
    for own, pieces in ((False, OTHER_PIECES), (True, OWN_PIECES)):
        done = [0, 0, 0]
        for m, size in pieces:
            half = core if own else 1 - core
            start = pl.multiple_of(half * (COLS[m] // 2) + done[m], LANES)
            cols = pl.ds(start, size)
            index = len(copies)
            group = []
            if done[m] == 0:
                whole = pl.ds(start, COLS[m] // 2)
                group.append(pltpu.make_async_copy(rights[m].at[:, whole], rbuf[m].at[:, whole], sems.at[index, 2]))
            group.append(pltpu.make_async_copy(grads[m].at[0, :, cols], gbuf[m].at[:, cols], sems.at[index, 0]))
            group.append(pltpu.make_async_copy(errors[m].at[0, :, cols], ebuf[m].at[:, cols], sems.at[index, 1]))
            for copy in group:
                copy.start()
            copies.append((own, m, start, FIRST_BLOCK[m] * BLOCK + done[m], size, group))
            done[m] += size
    totals = [tuple(jnp.zeros((ROWS, LANES), F32) for _ in range(RANK)) for _ in range(3)]
    for own, m, start, place, size, group in copies:
        for copy in group:
            copy.wait()

        def step(j, acc, own=own, m=m, start=start, place=place):
            cols = pl.ds(pl.multiple_of(start + j * LANES, LANES), LANES)
            value = gbuf[m][:, cols] + ebuf[m][:, cols].astype(F32)
            merged[m][:, cols] = value
            if not own:
                sent[:, pl.ds(pl.multiple_of(place + j * LANES, LANES), LANES)] = value
            return tuple(acc[i] + value * rbuf[m][i : i + 1, cols] for i in range(RANK))

        totals[m] = lax.fori_loop(0, size // LANES, step, totals[m], unroll=16)
    lanes = lane_iota(ROWS)
    result = jnp.zeros((ROWS, LANES), F32)
    for m in range(3):
        for i in range(RANK):
            column = jnp.sum(totals[m][i], axis=1, keepdims=True)
            result = jnp.where(lanes == m * RANK + i, column, result)
    partial[...] = result


def sum_replicas(parts):
    return ((parts[0][...] + parts[2][...]) + (parts[1][...] + parts[3][...])) * 0.125


def split_kernel(received, *refs):
    merged, parts = refs[0:3], refs[3]
    core = lax.rem(lax.axis_index("dp"), 2)
    for m in range(3):

        def step(j, carry, m=m):
            here = pl.ds(pl.multiple_of(FIRST_BLOCK[m] * BLOCK + j * LANES, LANES), LANES)
            mine = merged[m][:, pl.ds(pl.multiple_of(core * (COLS[m] // 2) + j * LANES, LANES), LANES)]
            value = mine + received[:, here]
            high = value.astype(BF16)
            parts[0:ROWS, here] = high
            parts[ROWS : 2 * ROWS, here] = (value - high.astype(F32)).astype(BF16)
            return carry

        lax.fori_loop(0, COLS[m] // 2 // LANES, step, 0, unroll=16)


def product_kernel(*refs):
    gathered, parts, out, square = refs[0:4], refs[4], refs[5], refs[6]
    left = sum_replicas(gathered)
    square[...] = jnp.zeros((LANES, LANES), F32)
    square[0:ROWS, :] = left
    turned = square[...].T[0 : 3 * RANK, 0:ROWS]
    high = turned.astype(BF16).astype(F32)
    low = turned - high
    for m in range(3):
        mine = slice(m * RANK, (m + 1) * RANK)
        factors = jnp.concatenate(
            [
                jnp.concatenate([high[mine], high[mine]], axis=1),
                jnp.concatenate([low[mine], low[mine]], axis=1),
            ],
            axis=0,
        ).astype(BF16)
        start = FIRST_BLOCK[m] * BLOCK
        both = jnp.dot(factors, parts[:, start : start + COLS[m] // 2], preferred_element_type=F32)
        for j in range(COLS[m] // 2 // LANES):
            place = FIRST_BLOCK[m] * 4 + j
            row = place // 4 * BLOCK_ROWS + place % 4 * RANK
            value = both[:, j * LANES : (j + 1) * LANES]
            out[row : row + RANK, :] = value[0:RANK] + value[RANK : 2 * RANK]
    lanes = lane_iota(1)
    gram = jnp.zeros((1, LANES), F32)
    for shift in range(RANK):
        other = left if shift == 0 else pltpu.roll(left, LANES - shift, 1)
        row = jnp.where(lanes < 3 * RANK, jnp.sum(left * other, axis=0, keepdims=True), 0.0)
        gram = gram + (row if shift == 0 else pltpu.roll(row, 16 * shift, 1))
    for k in range(CHIPS):
        out[k * BLOCK_ROWS + 16 : (k + 1) * BLOCK_ROWS, :] = gram


def solve_kernel(blocks, *refs):
    gathered, copies, left_out, scratch = refs[0:4], refs[4], refs[5], refs[6]
    total = [jnp.zeros((16, LANES), F32) for _ in range(4)]
    grams = [jnp.zeros((1, LANES), F32) for _ in range(4)]
    for k in range(CHIPS):
        total[k % 4] = total[k % 4] + blocks[k * BLOCK_ROWS : k * BLOCK_ROWS + 16, :]
        grams[k % 4] = grams[k % 4] + blocks[k * BLOCK_ROWS + 16 : k * BLOCK_ROWS + 17, :]
    scratch[0:16, :] = (total[0] + total[1]) + (total[2] + total[3])
    gram = ((grams[0] + grams[1]) + (grams[2] + grams[3])) * 0.25

    def entry(i, j):
        shift = 16 * (i - j) + j
        return gram if shift == 0 else pltpu.roll(gram, LANES - shift, 1)

    factor = {}
    for j in range(RANK):
        for i in range(j, RANK):
            value = entry(i, j)
            for k in range(j):
                value = value - factor[i, k] * factor[j, k]
            factor[i, j] = jnp.sqrt(value) if i == j else value / factor[j, j]

    left_sum = sum_replicas(gathered)
    lanes = lane_iota(ROWS)
    valid = (lanes < 3 * RANK) & ((lanes & 3) == 0)
    rows, left = [], jnp.zeros((ROWS, LANES), F32)
    for i in range(RANK):
        current = left_sum if i == 0 else pltpu.roll(left_sum, LANES - i, 1)
        for j in range(i):
            current = current - factor[i, j] * rows[j]
        rows.append(current / factor[i, i])
        kept = jnp.where(valid, rows[i], 0.0)
        left = left + (kept if i == 0 else pltpu.roll(kept, i, 1))
    left_out[...] = left

    tensor = lax.axis_index("tensor")
    x, z, y = lax.div(lax.axis_index("dp"), 2), lax.div(tensor, 4), lax.rem(tensor, 4)
    mine = lax.rem(6 - x, 4) * 16 + lax.rem(6 - z, 4) * 4 + lax.rem(6 - y, 4)
    matrix = jnp.where(mine < FIRST_BLOCK[1], 0, jnp.where(mine < FIRST_BLOCK[2], 1, 2))
    one_lane = lane_iota(1) == matrix * RANK
    nexts = []
    for i in range(RANK):
        current = scratch[pl.ds(i, 4, stride=4), :] * 0.125
        for j in range(i):
            value = jnp.sum(jnp.where(one_lane, factor[i, j], 0.0), axis=1, keepdims=True)
            current = current - value * nexts[j]
        value = jnp.sum(jnp.where(one_lane, factor[i, i], 0.0), axis=1, keepdims=True)
        nexts.append(current / value)
    for i in range(RANK):
        scratch[pl.ds(i, 4, stride=4), :] = nexts[i]
    block = scratch[0:16, :]
    for k in range(CHIPS):
        copies[16 * k : 16 * k + 16, :] = block


OUT_PIECES = (1, 1, 1)


def finish_kernel(own, *refs):
    rows, left_ref, merged = refs[0], refs[1], refs[2:5]
    if own:
        nexts, errors, lefts = refs[5:8], refs[8:11], refs[11:14]
        nbuf, ebuf, sems, square, lbuf, lsems = refs[14:17], refs[17:20], refs[20], refs[21], refs[22:25], refs[25]
    else:
        nexts, errors = refs[11:14], refs[14:17]
        nbuf, ebuf, sems = refs[17:20], refs[20:23], refs[23]
    core = lax.rem(lax.axis_index("dp"), 2)
    half = core if own else 1 - core
    left = left_ref[...]
    copies = []
    if own:
        square[...] = jnp.zeros((LANES, LANES), F32)
        square[0:ROWS, :] = left
        turned = square[...].T
        for m in range(3):
            lbuf[m][...] = turned[m * RANK : (m + 1) * RANK, 0:ROWS]
            copy = pltpu.make_async_copy(lbuf[m], lefts[m], lsems.at[m])
            copy.start()
            copies.append(copy)
    index = 0
    for m in range(3):
        size = COLS[m] // 2 // OUT_PIECES[m]
        columns = [
            jnp.broadcast_to(left[:, m * RANK + i : m * RANK + i + 1], (ROWS, LANES)) for i in range(RANK)
        ]
        for piece in range(OUT_PIECES[m]):

            def step(j, carry, m=m, piece=piece, columns=columns, size=size):
                row = FIRST_BLOCK[m] * 16 + piece * (size // LANES) * RANK + j * 8
                both = rows[pl.ds(pl.multiple_of(row, 8), 8), :]
                for b in range(2):
                    local = pl.multiple_of(piece * size + (2 * j + b) * LANES, LANES)
                    value = merged[m][:, pl.ds(pl.multiple_of(half * (COLS[m] // 2) + local, LANES), LANES)]
                    four = both[b * RANK : (b + 1) * RANK]
                    nbuf[m][:, pl.ds(local, LANES)] = four
                    approx = columns[0] * four[0:1]
                    for i in range(1, RANK):
                        approx = approx + columns[i] * four[i : i + 1]
                    ebuf[m][:, pl.ds(local, LANES)] = (value - approx).astype(BF16)
                return carry

            lax.fori_loop(0, size // LANES // 2, step, 0, unroll=8)
            here = pl.ds(piece * size, size)
            there = pl.ds(pl.multiple_of(half * (COLS[m] // 2) + piece * size, LANES), size)
            for copy in (
                pltpu.make_async_copy(ebuf[m].at[:, here], errors[m].at[0, :, there], sems.at[index, 0]),
                pltpu.make_async_copy(nbuf[m].at[:, here], nexts[m].at[:, there], sems.at[index, 1]),
            ):
                copy.start()
                copies.append(copy)
            index += 1
    for copy in copies:
        copy.wait()


ANY = pl.BlockSpec(memory_space=pl.ANY)
VMEM = pl.BlockSpec(memory_space=pltpu.VMEM)
PARAMS = pltpu.CompilerParams(vmem_limit_bytes=24 * 2**20)


def cost(flops, size):
    return pl.CostEstimate(flops=flops, bytes_accessed=size, transcendentals=0)


def per_device(*args):
    grads, errors, rights = args[0:3], args[3:6], args[6:9]
    grads, errors, rights = (
        [pltpu.with_memory_space_constraint(x, pltpu.HBM) for x in group] for group in (grads, errors, rights)
    )
    *merged, sent, partial = pl.pallas_call(
        merge_kernel,
        out_shape=[pltpu.VMEM((ROWS, c), F32) for c in COLS]
        + [jax.ShapeDtypeStruct((ROWS, HALF), F32), jax.ShapeDtypeStruct((ROWS, LANES), F32)],
        in_specs=[pl.BlockSpec(memory_space=pltpu.HBM)] * 9,
        out_specs=[VMEM] * 5,
        scratch_shapes=[pltpu.VMEM((ROWS, c), F32) for c in COLS]
        + [pltpu.VMEM((ROWS, c), BF16) for c in COLS]
        + [pltpu.VMEM((RANK, c), F32) for c in COLS]
        + [pltpu.SemaphoreType.DMA((len(OTHER_PIECES + OWN_PIECES), 3))],
        compiler_params=PARAMS,
        cost_estimate=cost(10**7, 7 * 2**20),
    )(*grads, *errors, *rights)
    swap = [(i, i ^ 1) for i in range(8)]
    chip_partial = partial + lax.ppermute(partial, "dp", swap)
    sent, chip_partial = lax.optimization_barrier((sent, chip_partial))
    received = lax.ppermute(sent, "dp", swap)
    gathered = [chip_partial] + [
        lax.ppermute(chip_partial, "dp", [(i, (i + 2 * k) % 8) for i in range(8)]) for k in range(1, 4)
    ]

    rows = CHIPS * BLOCK_ROWS
    parts = pl.pallas_call(
        split_kernel,
        out_shape=jax.ShapeDtypeStruct((2 * ROWS, HALF), BF16),
        in_specs=[VMEM] * 4,
        out_specs=VMEM,
        compiler_params=PARAMS,
        cost_estimate=cost(10**7, 6 * 2**20),
    )(received, *merged)
    chip_sum = pl.pallas_call(
        product_kernel,
        out_shape=jax.ShapeDtypeStruct((rows, LANES), F32),
        in_specs=[VMEM] * 5,
        out_specs=VMEM,
        scratch_shapes=[pltpu.VMEM((LANES, LANES), F32)],
        compiler_params=PARAMS,
        cost_estimate=cost(10**7, 3 * 2**20),
    )(*gathered, parts)
    both = ("dp", "tensor")
    down = (2, 1, 0, 3)
    chips = [[(2 * x + core) * 16 + z * 4 + y for x in down for z in down for y in down] for core in range(2)]
    blocks = lax.all_to_all(
        chip_sum.reshape(CHIPS, 1, BLOCK_ROWS * LANES), both, 0, 0, tiled=True, axis_index_groups=chips
    ).reshape(rows, LANES)

    copies, left = pl.pallas_call(
        solve_kernel,
        out_shape=[
            jax.ShapeDtypeStruct((CHIPS * 16, LANES), F32),
            jax.ShapeDtypeStruct((ROWS, LANES), F32),
        ],
        in_specs=[VMEM] * 5,
        out_specs=[VMEM] * 2,
        scratch_shapes=[pltpu.VMEM((24, LANES), F32)],
        compiler_params=PARAMS,
        cost_estimate=cost(10**6, 2**20),
    )(blocks, *gathered)
    mine = lax.all_to_all(
        copies.reshape(CHIPS, 1, 16 * LANES), both, 0, 0, tiled=True, axis_index_groups=chips
    ).reshape(CHIPS * 16, LANES)
    theirs = lax.ppermute(mine, "dp", swap)

    next_shapes = [jax.ShapeDtypeStruct((RANK, c), F32) for c in COLS]
    error_shapes = [jax.ShapeDtypeStruct((1, ROWS, c), BF16) for c in COLS]
    left_shapes = [jax.ShapeDtypeStruct((RANK, ROWS), F32)] * 3
    scratch = [pltpu.VMEM((RANK, c // 2), F32) for c in COLS] + [pltpu.VMEM((ROWS, c // 2), BF16) for c in COLS]
    sems = pltpu.SemaphoreType.DMA((sum(OUT_PIECES), 2))
    first = pl.pallas_call(
        functools.partial(finish_kernel, True),
        out_shape=next_shapes + error_shapes + left_shapes,
        in_specs=[VMEM] * 5,
        out_specs=[ANY] * 9,
        scratch_shapes=scratch
        + [sems, pltpu.VMEM((LANES, LANES), F32)]
        + [pltpu.VMEM((RANK, ROWS), F32)] * 3
        + [pltpu.SemaphoreType.DMA((3,))],
        compiler_params=PARAMS,
        cost_estimate=cost(10**7, 4 * 2**20),
    )(mine, left, *merged)
    lefts = first[6:9]
    second = pl.pallas_call(
        functools.partial(finish_kernel, False),
        out_shape=next_shapes + error_shapes,
        in_specs=[VMEM] * 5 + [ANY] * 6,
        out_specs=[ANY] * 6,
        scratch_shapes=scratch + [sems],
        input_output_aliases={5 + k: k for k in range(6)},
        compiler_params=PARAMS,
        cost_estimate=cost(10**7, 4 * 2**20),
    )(theirs, left, *merged, *first[0:6])
    return (*lefts, *second)


def solution(mesh):
    cut = P("dp", "tensor", None)
    return jax.shard_map(
        per_device,
        mesh=mesh,
        in_specs=(cut,) * 6 + (P(),) * 3,
        out_specs=(P(None, "tensor"),) * 3 + (P(),) * 3 + (cut,) * 3,
        check_vma=False,
    )
```
